128 devices in a mesh: row: 8 (over z, core), col: 16 (over y, x).
Axes of the slice: x: 4, y: 4, z: 4, core: 2. Of those that a mesh axis runs over, the one named last changes fastest.
Arguments:
- spectral: bfloat16 [3, 2, 5120, 7680], P(None, None, ('row', 'col')), may hold values from -6 to 6
- labels: int32 [2048, 2048], P(('row', 'col')), may hold values from 0 to 16383
- block_place: int32 [128], replicated, may hold values from 0 to 127, each once
Outputs:
- stats: float32 [6, 16, 1024], P(None, 'col', 'row')
The draws below stay inside these ranges and needn't reach their ends.
Inputs may be any that keep to these rules, and one draw needn't show every extreme that they name: `block_place`: each of 0 to 127 appears once.
All inputs are finite; a program needn't handle non-finite values.
Results may differ from the reference program's by a relative error of at most 0.00073.
Values may be sent and summed in bfloat16 or wider, within the bound.
A program may use at most 192 MiB of HBM per device.

```python
import math
import jax
import jax.numpy as jnp
import numpy as np
from jax import lax

KX = 5120
KZ = 7680
NX = 10240
ZW = 2048
XW = 2048
LB = 128
NBLK = 128
LABELS = 16384
N_COL = 16


def set_ends(array, stream_key, low, high):
    longest = array.shape.index(max(array.shape))
    spots = []
    for shift in (0, 1):
        where = [jax.random.randint(jax.random.fold_in(stream_key, axis), (), 0, length) for axis, length in enumerate(array.shape)]
        where[longest] = (where[longest] + shift) % array.shape[longest]
        spots.append(tuple(where))
    return array.at[spots[0]].set(low).at[spots[1]].set(high)


def steps_of(key, extent, split, least, top_value):
    def one(axis_at, blocks):
        steps = jax.random.uniform(jax.random.fold_in(jax.random.fold_in(key, 6), axis_at), (blocks,), jnp.float32, least / len(split), top_value / len(split))
        return jnp.repeat(jnp.exp(steps), extent[axis_at] // blocks).reshape((-1,) + (1,) * (len(extent) - axis_at - 1))

    level = one(*split[0])
    for cut in split[1:]:
        level = level * one(*cut)
    return level


def rank_table(number_of, lean):
    weights = [(1 << 20) // math.isqrt(grade ** lean) + 1 for grade in range(1, number_of + 1)]
    spread = 1 + sum(weights) // (1 << 30)
    return np.cumsum(np.array([max(1, weight // spread) for weight in weights]))


def ranked(key, dims, number_of, slope):
    grid = rank_table(number_of, slope)
    ticket = jax.random.randint(jax.random.fold_in(key, 1), dims, 0, int(grid[number_of - 1]))
    rank = jnp.searchsorted(jnp.asarray(grid, jnp.int32), ticket, side="right")
    return jax.random.permutation(jax.random.fold_in(key, 2), number_of)[rank].astype(jnp.int32)


def noise(key, extent, spread, bound, split=(), dtype=jnp.bfloat16):
    loudness = steps_of(key, extent, split, -0.22, 0.18) if split else 1.0
    values = jax.random.normal(key, extent, jnp.float32) * spread * loudness
    return jnp.minimum(jnp.maximum(values, -bound), bound).astype(dtype)


def setup_inputs(seed: int = 0) -> dict:
    key_list = jax.random.split(jax.random.key(seed), 4)
    spectral = noise(key_list[0], (3, 2, KX, KZ), 1.0, 6.0, ((2, 128),))
    labels = set_ends(ranked(key_list[1], (ZW, XW), LABELS, 2), jax.random.fold_in(key_list[1], 3), 0, LABELS - 1).astype(jnp.int32)
    block_place = jax.random.permutation(key_list[2], NBLK).astype(jnp.int32)
    return dict(spectral=spectral, labels=labels, block_place=block_place)


def wave_table(kvals, positions, modulus):
    phase = (kvals * positions % modulus).astype(jnp.float32) * (2.0 * math.pi / modulus)
    return (jnp.cos(phase), jnp.sin(phase))

def label_stats(enst, target, zstart, total):
    rows, cols = enst.shape
    zpos = (lax.broadcasted_iota(jnp.int32, (rows, cols), 0) + zstart).astype(jnp.float32) / ZW
    xpos = lax.broadcasted_iota(jnp.int32, (rows, cols), 1).astype(jnp.float32) / XW
    values = jnp.stack([jnp.ones_like(enst), enst, enst * xpos, enst * zpos, enst * xpos * xpos, enst * xpos * zpos, enst * zpos * zpos], 0)
    table = jnp.zeros((7, total), jnp.float32)
    return table.at[:, target.reshape(-1)].add(values.reshape(7, -1))

def finish(sums):
    weight = jnp.maximum(sums[1], 1.0)
    centre_x = sums[2] / weight
    centre_z = sums[3] / weight
    return jnp.stack([sums[1] / jnp.maximum(sums[0], 1.0), centre_x, centre_z, 12.0 * (sums[4] / weight - centre_x * centre_x), 12.0 * (sums[5] / weight - centre_x * centre_z), 12.0 * (sums[6] / weight - centre_z * centre_z)], 0)

def reference(spectral, labels, block_place):
    kvals = lax.broadcasted_iota(jnp.int32, (KZ, 1), 0)
    positions = lax.broadcasted_iota(jnp.int32, (1, ZW), 1)
    zcos, zsin = wave_table(kvals, positions, KZ)
    zcos = zcos.astype(jnp.bfloat16).astype(jnp.float32)
    zsin = zsin.astype(jnp.bfloat16).astype(jnp.float32)
    kx_vals = lax.broadcasted_iota(jnp.int32, (KX, 1), 0)
    xposit = lax.broadcasted_iota(jnp.int32, (1, XW), 1)
    xcos, xsin = wave_table(kx_vals, xposit, NX)
    weight = jnp.where(kx_vals == 0, 1.0, 2.0).astype(jnp.float32)
    xcos = (weight * xcos).astype(jnp.bfloat16).astype(jnp.float32)
    xsin = (weight * xsin).astype(jnp.bfloat16).astype(jnp.float32)
    scale = 1.0 / math.sqrt(2.0 * KX * KZ)
    enst = jnp.zeros((ZW, XW), jnp.float32)
    for comp in range(3):
        real_in = spectral[comp, 0].astype(jnp.float32)
        imag_in = spectral[comp, 1].astype(jnp.float32)
        pcos_re = jnp.dot(real_in, zcos, preferred_element_type=jnp.float32)
        psin_im = jnp.dot(imag_in, zsin, preferred_element_type=jnp.float32)
        zreal = (pcos_re - psin_im).astype(jnp.bfloat16).astype(jnp.float32)
        psin_re = jnp.dot(real_in, zsin, preferred_element_type=jnp.float32)
        pcos_im = jnp.dot(imag_in, zcos, preferred_element_type=jnp.float32)
        zimag = (psin_re + pcos_im).astype(jnp.bfloat16).astype(jnp.float32)
        value = jnp.einsum('kz,kx->zx', zreal, xcos) - jnp.einsum('kz,kx->zx', zimag, xsin)
        value = value * scale
        enst = enst + value * value
    target = jnp.take(block_place, labels // LB) * LB + labels % LB
    sums = label_stats(enst, target.astype(jnp.int32), 0, NBLK * LB)
    result = finish(sums)
    return result.reshape(6, N_COL, NBLK * LB // N_COL)
```

```python
import math

import jax
import jax.numpy as jnp
import ml_dtypes
import numpy as np
from jax import lax
from jax.experimental import pallas as pl
from jax.experimental.pallas import tpu as pltpu
from jax.sharding import PartitionSpec as P

KX = 5120
KZ = 7680
NX = 10240
ZW = 2048
XW = 2048
ND = 128
MODES = 40
QK = KZ // 4
ROWS = 16
LANES = 128
NT = (((1,), (1,)), ((), ()))
VMEM_LIMIT = 60 * 1024 * 1024


def split(table):
    high = table.astype(ml_dtypes.bfloat16)
    low = (table - high.astype(np.float64)).astype(ml_dtypes.bfloat16)
    return high, low


def z_table():
    za = np.arange(4)[:, None, None]
    zq = np.arange(4)[None, :, None]
    d = np.arange(ND)[None, None, :]
    z = (16 * d + 4 * zq + za).reshape(4, 512)
    cycle = (np.arange(KZ).astype(np.float32) * np.float32(2.0 * math.pi / KZ)).astype(np.float32)
    cosine = np.cos(cycle).astype(ml_dtypes.bfloat16)
    sine = np.sin(cycle).astype(ml_dtypes.bfloat16)
    phase = (z[:, :, None] * np.arange(QK)[None, None, :]) % KZ
    return np.concatenate([cosine[phase], sine[phase]], 1)


def x_tables():
    s = np.arange(ND)
    xa = np.arange(256)
    angle = 2.0 * math.pi * ((xa[:, None] * s[None, :]) % 256) / 256
    real_rows = np.concatenate([np.cos(angle), -np.sin(angle)], 1)
    imag_rows = np.concatenate([np.sin(angle), np.cos(angle)], 1)
    first = np.stack(split(np.concatenate([real_rows, imag_rows], 0)))
    m = np.zeros(LANES, np.int64)
    m[: 3 * MODES] = np.arange(3 * MODES) % MODES
    angle = 2.0 * math.pi * (xa[:, None] * m[None, :]) / NX
    twiddle = np.stack([np.cos(angle), np.sin(angle)]).astype(np.float32)
    xb = np.arange(8)
    last = np.zeros((3, 8, 2, LANES))
    for c in range(3):
        angle = 2.0 * math.pi * ((xb[:, None] * np.arange(MODES)[None, :]) % MODES) / MODES
        last[c, :, 0, c * MODES : (c + 1) * MODES] = np.cos(angle)
        last[c, :, 1, c * MODES : (c + 1) * MODES] = -np.sin(angle)
    last = last.reshape(24, 2 * LANES)
    high, low = split(last)
    last = np.concatenate([high, low], 0)
    return first, twiddle, last


def z_kernel(spec_ref, tab_ref, out_ref, preal, pimag, high, low):
    za = pl.program_id(0)
    width = 640

    def fill(residue):
        for start in range(0, QK, width):
            reals, imags = [], []
            for c in range(3):
                quarter = [
                    [
                        spec_ref[2 * c + part, :, ka * QK + start : ka * QK + start + width].astype(jnp.float32)
                        for ka in range(4)
                    ]
                    for part in range(2)
                ]
                (r0, r1, r2, r3), (i0, i1, i2, i3) = quarter
                if residue % 2 == 0:
                    pr, pi, qr, qi = r0 + r2, i0 + i2, r1 + r3, i1 + i3
                else:
                    pr, pi, qr, qi = r0 - r2, i0 - i2, r1 - r3, i1 - i3
                if residue == 0:
                    re, im = pr + qr, pi + qi
                elif residue == 1:
                    re, im = pr - qi, pi + qr
                elif residue == 2:
                    re, im = pr - qr, pi - qi
                else:
                    re, im = pr + qi, pi - qr
                reals.append(re)
                imags.append(im)
            pad = jnp.zeros((LANES - 3 * MODES, width), jnp.float32)
            for part, pieces in enumerate((reals, imags)):
                whole = jnp.concatenate(pieces + [pad], 0)
                top = whole.astype(jnp.bfloat16)
                rest = (whole - top.astype(jnp.float32)).astype(jnp.bfloat16)
                high[part * LANES : (part + 1) * LANES, start : start + width] = top
                low[part * LANES : (part + 1) * LANES, start : start + width] = rest

    for residue in range(4):
        pl.when(za == residue)(lambda residue=residue: fill(residue))

    for zq in range(4):
        sums = []
        for part in range(2):
            rows = tab_ref[0, part * 512 + zq * ND : part * 512 + (zq + 1) * ND, :]
            sums.append(
                lax.dot_general(rows, high[...], NT, preferred_element_type=jnp.float32)
                + lax.dot_general(rows, low[...], NT, preferred_element_type=jnp.float32)
            )
        cosine, sine = sums
        real = cosine[:, :LANES] - sine[:, LANES:]
        imag = sine[:, :LANES] + cosine[:, LANES:]
        preal[pl.ds(za * 4 + zq, ND, stride=ROWS), :] = real
        pimag[pl.ds(za * 4 + zq, ND, stride=ROWS), :] = imag

    @pl.when(za == 3)
    def _():
        out_ref[:, :LANES] = preal[...].astype(jnp.bfloat16)
        out_ref[:, LANES:] = pimag[...].astype(jnp.bfloat16)


def z_transform(spec, table):
    return pl.pallas_call(
        z_kernel,
        out_shape=jax.ShapeDtypeStruct((ND * ROWS, 2 * LANES), jnp.bfloat16),
        grid=(4,),
        in_specs=[
            pl.BlockSpec((6, MODES, KZ), lambda i: (0, 0, 0)),
            pl.BlockSpec((1, 1024, QK), lambda i: (i, 0, 0)),
        ],
        out_specs=pl.BlockSpec((ND * ROWS, 2 * LANES), lambda i: (0, 0)),
        scratch_shapes=[
            pltpu.VMEM((ND * ROWS, LANES), jnp.float32),
            pltpu.VMEM((ND * ROWS, LANES), jnp.float32),
            pltpu.VMEM((2 * LANES, QK), jnp.bfloat16),
            pltpu.VMEM((2 * LANES, QK), jnp.bfloat16),
        ],
        compiler_params=pltpu.CompilerParams(vmem_limit_bytes=VMEM_LIMIT),
    )(spec, table)


def zpoint(i):
    return 4 * (i % 4) + i // 4


def x_kernel(me_ref, place_ref, recv_ref, lab_ref, first_ref, tw_ref, last_ref, out_ref, wreal, wimag, enst, acc0, acc1, lhs, rhs):
    scale = 2.0 / math.sqrt(2.0 * KX * KZ)
    wreal[...] = recv_ref[:, :LANES].astype(jnp.float32)
    wimag[...] = recv_ref[:, LANES:].astype(jnp.float32)
    lane = lax.broadcasted_iota(jnp.int32, (ROWS, LANES), 1)
    factor = jnp.where((lane == 0) | (lane == MODES) | (lane == 2 * MODES), 0.5, 1.0)
    wreal[0:ROWS, :] = wreal[0:ROWS, :] * factor
    wimag[0:ROWS, :] = wimag[0:ROWS, :] * factor

    def transform(pair, carry):
        sides = []
        for half in range(2):
            rows = pl.ds(pair * 2 + half, ND, stride=ROWS)
            sides.append(jnp.concatenate([wreal[rows, :], wimag[rows, :]], 0))
        both = jnp.concatenate(sides, 1).astype(jnp.bfloat16)
        y = jnp.dot(first_ref[0], both, preferred_element_type=jnp.float32) + jnp.dot(
            first_ref[1], both, preferred_element_type=jnp.float32
        )
        cosine, sine = tw_ref[0], tw_ref[1]
        for half in range(2):
            yr = y[0:256, half * LANES : (half + 1) * LANES]
            yi = y[256:512, half * LANES : (half + 1) * LANES]
            t = jnp.concatenate([yr * cosine - yi * sine, yr * sine + yi * cosine], 1)
            top = t.astype(jnp.bfloat16)
            rest = (t - top.astype(jnp.float32)).astype(jnp.bfloat16)
            v = lax.dot_general(last_ref[...], top, NT, preferred_element_type=jnp.float32)
            v = v[0:24] + v[24:48]
            v = v + lax.dot_general(last_ref[0:24], rest, NT, preferred_element_type=jnp.float32)
            v = v * scale
            enst[pair * 2 + half] = v[0:8] * v[0:8] + v[8:16] * v[8:16] + v[16:24] * v[16:24]
        return carry

    lax.fori_loop(0, ROWS // 2, transform, 0)

    acc0[...] = jnp.zeros_like(acc0)
    acc1[...] = jnp.zeros_like(acc1)
    upos = (
        lax.broadcasted_iota(jnp.int32, (8, 256), 0) * 256 + lax.broadcasted_iota(jnp.int32, (8, 256), 1)
    ).astype(jnp.float32) / XW - 0.5
    row64 = lax.broadcasted_iota(jnp.int32, (64, 256), 0)
    row256 = lax.broadcasted_iota(jnp.int32, (256, 256), 0)

    def gather(i, carry):
        z = zpoint(i)
        e = enst[i]
        ehigh = e.astype(jnp.bfloat16).astype(jnp.float32)
        eu = e * upos
        values = [jnp.ones_like(e), ehigh, e - ehigh, eu, eu * upos]
        for xb in range(8):
            cols = slice(xb * 256, (xb + 1) * 256)
            lab = lab_ref[pl.ds(z, 1), cols]
            hit = jnp.broadcast_to(lab >> 8, (64, 256)) == row64
            for j, value in enumerate(values):
                picked = jnp.where(hit, jnp.broadcast_to(value[xb : xb + 1], (64, 256)), 0.0)
                lhs[j * 64 : (j + 1) * 64, cols] = picked.astype(jnp.bfloat16)
            near = jnp.broadcast_to(lab & 255, (256, 256)) == row256
            rhs[:, cols] = jnp.where(near, 1.0, 0.0).astype(jnp.bfloat16)
        t = lax.dot_general(lhs[...], rhs[...], NT, preferred_element_type=jnp.float32)
        w = (me_ref[0] * ROWS + z).astype(jnp.float32) / ZW - 0.5
        e_sum = t[64:128] + t[128:192]
        eu_sum = t[192:256]
        terms = [t[0:64], e_sum, eu_sum, e_sum * w, t[256:320], eu_sum * w, e_sum * (w * w)]
        for j, term in enumerate(terms):
            acc0[j * 64 : (j + 1) * 64, :] += term[:, :128]
            acc1[j * 64 : (j + 1) * 64, :] += term[:, 128:]
        return carry

    lax.fori_loop(0, ROWS, gather, 0)

    for b in range(128):
        place = place_ref[b]
        owner = (place % 8) * 16 + place // 8
        out_ref[owner] = (acc0, acc1)[b % 2][pl.ds(b // 2, 8, stride=64), :]


def x_transform(me, place, recv, labels, first, twiddle, last):
    vmem = pl.BlockSpec(memory_space=pltpu.VMEM)
    smem = pl.BlockSpec(memory_space=pltpu.SMEM)
    return pl.pallas_call(
        x_kernel,
        out_shape=jax.ShapeDtypeStruct((ND, 8, 128), jnp.float32),
        in_specs=[smem, smem, vmem, vmem, vmem, vmem, vmem],
        out_specs=vmem,
        scratch_shapes=[
            pltpu.VMEM((ND * ROWS, LANES), jnp.float32),
            pltpu.VMEM((ND * ROWS, LANES), jnp.float32),
            pltpu.VMEM((ROWS, 8, 256), jnp.float32),
            pltpu.VMEM((512, 128), jnp.float32),
            pltpu.VMEM((512, 128), jnp.float32),
            pltpu.VMEM((320, XW), jnp.bfloat16),
            pltpu.VMEM((256, XW), jnp.bfloat16),
        ],
        compiler_params=pltpu.CompilerParams(vmem_limit_bytes=VMEM_LIMIT),
    )(me, place, recv, labels, first, twiddle, last)


def finish(centred):
    count, s1, u1, w1, uu, uw, ww = (centred[j] for j in range(7))
    s2 = u1 + 0.5 * s1
    s3 = w1 + 0.5 * s1
    s4 = uu + u1 + 0.25 * s1
    s5 = uw + 0.5 * (u1 + w1) + 0.25 * s1
    s6 = ww + w1 + 0.25 * s1
    weight = jnp.maximum(s1, 1.0)
    centre_x = s2 / weight
    centre_z = s3 / weight
    return jnp.stack(
        [
            s1 / jnp.maximum(count, 1.0),
            centre_x,
            centre_z,
            12.0 * (s4 / weight - centre_x * centre_x),
            12.0 * (s5 / weight - centre_x * centre_z),
            12.0 * (s6 / weight - centre_z * centre_z),
        ],
        0,
    )


def solution(mesh):
    table = z_table()
    first, twiddle, last = x_tables()

    def on_device(spectral, labels, block_place):
        me = lax.axis_index("row") * lax.axis_size("col") + lax.axis_index("col")
        msg = z_transform(spectral.reshape(6, MODES, KZ), table)
        msg = msg.reshape(ND, ROWS, 2 * LANES)
        recv = lax.all_to_all(msg, ("row", "col"), split_axis=0, concat_axis=0, tiled=True)
        sums = x_transform(
            me.reshape(1), block_place, recv.reshape(ND * ROWS, 2 * LANES), labels, first, twiddle, last
        )
        parts = lax.all_to_all(sums, ("row", "col"), split_axis=0, concat_axis=0, tiled=True)
        return finish(jnp.sum(parts, axis=0)).reshape(6, 1, 128)

    in_specs = (P(None, None, ("row", "col"), None), P(("row", "col"), None), P())
    return jax.shard_map(on_device, mesh=mesh, in_specs=in_specs, out_specs=P(None, "col", "row"), check_vma=False)
```

```python
import math

import jax
import jax.numpy as jnp
import ml_dtypes
import numpy as np
from jax import lax
from jax.experimental import pallas as pl
from jax.experimental.pallas import tpu as pltpu
from jax.sharding import PartitionSpec as P

KX = 5120
KZ = 7680
NX = 10240
ZW = 2048
XW = 2048
ND = 128
MODES = 40
QK = KZ // 4
ROWS = 16
LANES = 128
MESH = pl.DeviceIdType.MESH
NT = (((1,), (1,)), ((), ()))
VMEM_LIMIT = 60 * 1024 * 1024


def split(table):
    high = table.astype(ml_dtypes.bfloat16)
    low = (table - high.astype(np.float64)).astype(ml_dtypes.bfloat16)
    return high, low


def z_table():
    za = np.arange(4)[:, None, None]
    zq = np.arange(4)[None, :, None]
    d = np.arange(ND)[None, None, :]
    z = (16 * d + 4 * zq + za).reshape(4, 512)
    cycle = (np.arange(KZ).astype(np.float32) * np.float32(2.0 * math.pi / KZ)).astype(np.float32)
    cosine = np.cos(cycle).astype(ml_dtypes.bfloat16)
    sine = np.sin(cycle).astype(ml_dtypes.bfloat16)
    phase = (z[:, :, None] * np.arange(QK)[None, None, :]) % KZ
    return np.concatenate([cosine[phase], sine[phase]], 1)


def x_tables():
    s = np.arange(ND)
    xa = np.arange(256)
    angle = 2.0 * math.pi * ((xa[:, None] * s[None, :]) % 256) / 256
    real_rows = np.concatenate([np.cos(angle), -np.sin(angle)], 1)
    imag_rows = np.concatenate([np.sin(angle), np.cos(angle)], 1)
    first = np.concatenate(split(np.concatenate([real_rows, imag_rows], 0)), 1)
    m = np.zeros(LANES, np.int64)
    m[: 3 * MODES] = np.arange(3 * MODES) % MODES
    angle = 2.0 * math.pi * (xa[:, None] * m[None, :]) / NX
    twiddle = np.stack([np.cos(angle), np.sin(angle)]).astype(np.float32)
    xb = np.arange(8)
    last = np.zeros((3, 8, 2, LANES))
    for c in range(3):
        angle = 2.0 * math.pi * ((xb[:, None] * np.arange(MODES)[None, :]) % MODES) / MODES
        last[c, :, 0, c * MODES : (c + 1) * MODES] = np.cos(angle)
        last[c, :, 1, c * MODES : (c + 1) * MODES] = -np.sin(angle)
    last = last.reshape(24, 2 * LANES)
    high, low = split(last)
    last = np.concatenate([high, low], 0)
    return first, twiddle, last


def z_kernel(spec_ref, tab_ref, out_ref, preal, pimag, high, low):
    za = pl.program_id(0)
    width = 640

    def fill(residue):
        for start in range(0, QK, width):
            reals, imags = [], []
            for c in range(3):
                quarter = [
                    [
                        spec_ref[2 * c + part, :, ka * QK + start : ka * QK + start + width].astype(jnp.float32)
                        for ka in range(4)
                    ]
                    for part in range(2)
                ]
                (r0, r1, r2, r3), (i0, i1, i2, i3) = quarter
                if residue % 2 == 0:
                    pr, pi, qr, qi = r0 + r2, i0 + i2, r1 + r3, i1 + i3
                else:
                    pr, pi, qr, qi = r0 - r2, i0 - i2, r1 - r3, i1 - i3
                if residue == 0:
                    re, im = pr + qr, pi + qi
                elif residue == 1:
                    re, im = pr - qi, pi + qr
                elif residue == 2:
                    re, im = pr - qr, pi - qi
                else:
                    re, im = pr + qi, pi - qr
                reals.append(re)
                imags.append(im)
            pad = jnp.zeros((LANES - 3 * MODES, width), jnp.float32)
            for part, pieces in enumerate((reals, imags)):
                whole = jnp.concatenate(pieces + [pad], 0)
                top = whole.astype(jnp.bfloat16)
                rest = (whole - top.astype(jnp.float32)).astype(jnp.bfloat16)
                high[part * LANES : (part + 1) * LANES, start : start + width] = top
                low[part * LANES : (part + 1) * LANES, start : start + width] = rest

    for residue in range(4):
        pl.when(za == residue)(lambda residue=residue: fill(residue))

    for zq in range(4):
        sums = []
        for part in range(2):
            rows = tab_ref[0, part * 512 + zq * ND : part * 512 + (zq + 1) * ND, :]
            sums.append(
                lax.dot_general(rows, high[...], NT, preferred_element_type=jnp.float32)
                + lax.dot_general(rows, low[...], NT, preferred_element_type=jnp.float32)
            )
        cosine, sine = sums
        real = cosine[:, :LANES] - sine[:, LANES:]
        imag = sine[:, :LANES] + cosine[:, LANES:]
        preal[pl.ds(za * 4 + zq, ND, stride=ROWS), :] = real
        pimag[pl.ds(za * 4 + zq, ND, stride=ROWS), :] = imag

    @pl.when(za == 3)
    def _():
        out_ref[:, :LANES] = preal[...].astype(jnp.bfloat16)
        out_ref[:, LANES:] = pimag[...].astype(jnp.bfloat16)


def z_transform(spec, table):
    return pl.pallas_call(
        z_kernel,
        out_shape=jax.ShapeDtypeStruct((ND * ROWS, 2 * LANES), jnp.bfloat16),
        grid=(4,),
        in_specs=[
            pl.BlockSpec((6, MODES, KZ), lambda i: (0, 0, 0)),
            pl.BlockSpec((1, 1024, QK), lambda i: (i, 0, 0)),
        ],
        out_specs=pl.BlockSpec((ND * ROWS, 2 * LANES), lambda i: (0, 0)),
        scratch_shapes=[
            pltpu.VMEM((ND * ROWS, LANES), jnp.float32),
            pltpu.VMEM((ND * ROWS, LANES), jnp.float32),
            pltpu.VMEM((2 * LANES, QK), jnp.bfloat16),
            pltpu.VMEM((2 * LANES, QK), jnp.bfloat16),
        ],
        compiler_params=pltpu.CompilerParams(vmem_limit_bytes=VMEM_LIMIT),
    )(spec, table)


def zpoint(i):
    return 4 * (i % 4) + i // 4


def spread(row, count):
    tile = jnp.broadcast_to(row, (16, row.shape[1])).astype(jnp.bfloat16)
    return jnp.concatenate([tile] * (count // 16), 0)


def x_kernel(
    me_ref, place_ref, recv_ref, lab_ref, first_ref, tw_ref, last_ref, out_ref,
    wreal, wimag, mats, top, rest, enst, acc0, acc1, lhs_a, rhs_a, lhs_b, rhs_b,
):
    scale = 2.0 / math.sqrt(2.0 * KX * KZ)
    wreal[...] = recv_ref[:, :LANES].astype(jnp.float32)
    wimag[...] = recv_ref[:, LANES:].astype(jnp.float32)
    lane = lax.broadcasted_iota(jnp.int32, (ROWS, LANES), 1)
    factor = jnp.where((lane == 0) | (lane == MODES) | (lane == 2 * MODES), 0.5, 1.0)
    wreal[0:ROWS, :] = wreal[0:ROWS, :] * factor
    wimag[0:ROWS, :] = wimag[0:ROWS, :] * factor
    for i in range(ROWS):
        rows = pl.ds(i, ND, stride=ROWS)
        cols = slice(i * LANES, (i + 1) * LANES)
        for part, wide in enumerate((wreal, wimag)):
            mat = wide[rows, :].astype(jnp.bfloat16)
            mats[part * ND : (part + 1) * ND, cols] = mat
            mats[(part + 2) * ND : (part + 3) * ND, cols] = mat

    cosine, sine = tw_ref[0], tw_ref[1]
    for pair in range(ROWS // 2):
        both = mats[:, pair * 256 : (pair + 1) * 256]
        y = jnp.dot(first_ref[...], both, preferred_element_type=jnp.float32)
        for half in range(2):
            yr = y[0:256, half * LANES : (half + 1) * LANES]
            yi = y[256:512, half * LANES : (half + 1) * LANES]
            t = jnp.concatenate([yr * cosine - yi * sine, yr * sine + yi * cosine], 1)
            high = t.astype(jnp.bfloat16)
            rows = slice((pair * 2 + half) * 256, (pair * 2 + half + 1) * 256)
            top[rows, :] = high
            rest[rows, :] = (t - high.astype(jnp.float32)).astype(jnp.bfloat16)
    v = lax.dot_general(last_ref[...], top[...], NT, preferred_element_type=jnp.float32)
    v = v[0:24] + v[24:48]
    v = v + lax.dot_general(last_ref[0:24], rest[...], NT, preferred_element_type=jnp.float32)
    v = v * scale
    enst[...] = v[0:8] * v[0:8] + v[8:16] * v[8:16] + v[16:24] * v[16:24]

    acc0[...] = jnp.zeros_like(acc0)
    acc1[...] = jnp.zeros_like(acc1)
    upos = (
        lax.broadcasted_iota(jnp.int32, (8, 256), 0) * 256 + lax.broadcasted_iota(jnp.int32, (8, 256), 1)
    ).astype(jnp.float32) / XW - 0.5
    row64 = lax.broadcasted_iota(jnp.int32, (64, 256), 0).astype(jnp.float32).astype(jnp.bfloat16)
    row256 = lax.broadcasted_iota(jnp.int32, (256, 256), 0).astype(jnp.float32).astype(jnp.bfloat16)
    one = jnp.ones((), jnp.bfloat16)
    zero = jnp.zeros((), jnp.bfloat16)

    def build(i, lhs, rhs):
        z = zpoint(i)
        e = enst[:, pl.ds(pl.multiple_of(i * 256, 256), 256)]
        ehigh = e.astype(jnp.bfloat16).astype(jnp.float32)
        eu = e * upos
        values = [ehigh, e - ehigh, eu, eu * upos]
        for xb in range(8):
            cols = slice(xb * 256, (xb + 1) * 256)
            lab = lab_ref[pl.ds(z, 1), cols]
            hit = spread((lab >> 8).astype(jnp.float32), 64) == row64
            lhs[0:64, cols] = jnp.where(hit, one, zero)
            for j, value in enumerate(values):
                lhs[(j + 1) * 64 : (j + 2) * 64, cols] = jnp.where(hit, spread(value[xb : xb + 1], 64), zero)
            near = spread((lab & 255).astype(jnp.float32), 256) == row256
            rhs[:, cols] = jnp.where(near, one, zero)

    def collect(i, lhs, rhs):
        t = lax.dot_general(lhs[...], rhs[...], NT, preferred_element_type=jnp.float32)
        w = (me_ref[0] * ROWS + zpoint(i)).astype(jnp.float32) / ZW - 0.5
        e_sum = t[64:128] + t[128:192]
        eu_sum = t[192:256]
        terms = [t[0:64], e_sum, eu_sum, e_sum * w, t[256:320], eu_sum * w, e_sum * (w * w)]
        for j, term in enumerate(terms):
            acc0[j * 64 : (j + 1) * 64, :] += term[:, :128]
            acc1[j * 64 : (j + 1) * 64, :] += term[:, 128:]

    build(0, lhs_a, rhs_a)

    def two_rows(n, carry):
        build(2 * n + 1, lhs_b, rhs_b)
        collect(2 * n, lhs_a, rhs_a)
        build(lax.rem(2 * n + 2, ROWS), lhs_a, rhs_a)
        collect(2 * n + 1, lhs_b, rhs_b)
        return carry

    lax.fori_loop(0, ROWS // 2, two_rows, 0)

    for b in range(128):
        place = place_ref[b]
        owner = (place % 2) * 64 + (place % 8) // 2 * 16 + place // 8
        out_ref[owner] = (acc0, acc1)[b % 2][pl.ds(b // 2, 8, stride=64), :]


def x_transform(me, place, recv, labels, first, twiddle, last):
    vmem = pl.BlockSpec(memory_space=pltpu.VMEM)
    smem = pl.BlockSpec(memory_space=pltpu.SMEM)
    return pl.pallas_call(
        x_kernel,
        out_shape=jax.ShapeDtypeStruct((ND, 8, 128), jnp.float32),
        in_specs=[smem, smem, vmem, vmem, vmem, vmem, vmem],
        out_specs=vmem,
        scratch_shapes=[
            pltpu.VMEM((ND * ROWS, LANES), jnp.float32),
            pltpu.VMEM((ND * ROWS, LANES), jnp.float32),
            pltpu.VMEM((512, ROWS * LANES), jnp.bfloat16),
            pltpu.VMEM((ROWS * 256, 2 * LANES), jnp.bfloat16),
            pltpu.VMEM((ROWS * 256, 2 * LANES), jnp.bfloat16),
            pltpu.VMEM((8, ROWS * 256), jnp.float32),
            pltpu.VMEM((512, 128), jnp.float32),
            pltpu.VMEM((512, 128), jnp.float32),
            pltpu.VMEM((320, XW), jnp.bfloat16),
            pltpu.VMEM((256, XW), jnp.bfloat16),
            pltpu.VMEM((320, XW), jnp.bfloat16),
            pltpu.VMEM((256, XW), jnp.bfloat16),
        ],
        compiler_params=pltpu.CompilerParams(vmem_limit_bytes=VMEM_LIMIT),
    )(me, place, recv, labels, first, twiddle, last)


def owner_of(core, q):
    return (q // 16 * 2 + core, q % 16)


def sum_kernel(sums_ref, out_ref, mate, part, parts, pair_send, pair_recv, send_sem, recv_sem):
    row = lax.axis_index("row")
    col = lax.axis_index("col")
    core = row % 2
    mine = row // 2 * 16 + col
    barrier = pltpu.get_barrier_semaphore()
    other = (row + 1 - 2 * core, col)
    pl.semaphore_signal(barrier, inc=1, device_id=other, device_id_type=MESH)

    def greet(j, carry):
        pl.semaphore_signal(barrier, inc=1, device_id=owner_of(core, lax.rem(mine + j, 64)), device_id_type=MESH)
        return carry

    lax.fori_loop(1, 64, greet, 0)
    pl.semaphore_wait(barrier, 64)
    swap = pltpu.make_async_remote_copy(
        src_ref=sums_ref.at[pl.ds((1 - core) * 64, 64)],
        dst_ref=mate,
        send_sem=pair_send,
        recv_sem=pair_recv,
        device_id=other,
        device_id_type=MESH,
    )
    swap.start()
    swap.wait()
    part[...] = sums_ref[pl.ds(core * 64, 64)] + mate[...]

    def send(j, carry):
        q = lax.rem(mine + j, 64)
        pltpu.make_async_remote_copy(
            src_ref=part.at[q],
            dst_ref=parts.at[mine],
            send_sem=send_sem,
            recv_sem=recv_sem,
            device_id=owner_of(core, q),
            device_id_type=MESH,
        ).start()
        return carry

    lax.fori_loop(1, 64, send, 0)
    parts[mine] = part[mine]
    every = parts.at[pl.ds(0, 63)]
    pltpu.make_async_copy(part.at[pl.ds(0, 63)], every, send_sem).wait()
    pltpu.make_async_copy(every, every, recv_sem).wait()
    out_ref[...] = finish(jnp.sum(parts[...], 0))


def sum_up(sums):
    vmem = pl.BlockSpec(memory_space=pltpu.VMEM)
    return pl.pallas_call(
        sum_kernel,
        out_shape=jax.ShapeDtypeStruct((6, 128), jnp.float32),
        in_specs=[vmem],
        out_specs=vmem,
        scratch_shapes=[
            pltpu.VMEM((64, 8, 128), jnp.float32),
            pltpu.VMEM((64, 8, 128), jnp.float32),
            pltpu.VMEM((64, 8, 128), jnp.float32),
        ]
        + [pltpu.SemaphoreType.DMA] * 4,
        compiler_params=pltpu.CompilerParams(collective_id=1, has_side_effects=True),
    )(sums)


def finish(centred):
    count, s1, u1, w1, uu, uw, ww = (centred[j] for j in range(7))
    s2 = u1 + 0.5 * s1
    s3 = w1 + 0.5 * s1
    s4 = uu + u1 + 0.25 * s1
    s5 = uw + 0.5 * (u1 + w1) + 0.25 * s1
    s6 = ww + w1 + 0.25 * s1
    weight = jnp.maximum(s1, 1.0)
    centre_x = s2 / weight
    centre_z = s3 / weight
    return jnp.stack(
        [
            s1 / jnp.maximum(count, 1.0),
            centre_x,
            centre_z,
            12.0 * (s4 / weight - centre_x * centre_x),
            12.0 * (s5 / weight - centre_x * centre_z),
            12.0 * (s6 / weight - centre_z * centre_z),
        ],
        0,
    )


def solution(mesh):
    table = z_table()
    first, twiddle, last = x_tables()

    def on_device(spectral, labels, block_place):
        me = lax.axis_index("row") * lax.axis_size("col") + lax.axis_index("col")
        msg = z_transform(spectral.reshape(6, MODES, KZ), table)
        msg = msg.reshape(ND, ROWS, 2 * LANES)
        recv = lax.all_to_all(msg, ("row", "col"), split_axis=0, concat_axis=0, tiled=True)
        sums = x_transform(
            me.reshape(1), block_place, recv.reshape(ND * ROWS, 2 * LANES), labels, first, twiddle, last
        )
        return sum_up(sums).reshape(6, 1, 128)

    in_specs = (P(None, None, ("row", "col"), None), P(("row", "col"), None), P())
    return jax.shard_map(on_device, mesh=mesh, in_specs=in_specs, out_specs=P(None, "col", "row"), check_vma=False)
```

```python
import math

import jax
import jax.numpy as jnp
import ml_dtypes
import numpy as np
from jax import lax
from jax.experimental import pallas as pl
from jax.experimental.pallas import tpu as pltpu
from jax.sharding import PartitionSpec as P

KX = 5120
KZ = 7680
NX = 10240
ZW = 2048
XW = 2048
ND = 128
MODES = 40
QK = KZ // 4
HALF = 1024
ROWS = 16
LB = 128
NBLK = 128
LANES = 128
MESH = pl.DeviceIdType.MESH
NT = (((1,), (1,)), ((), ()))
VMEM_LIMIT = 60 * 1024 * 1024


def split(table):
    high = table.astype(ml_dtypes.bfloat16)
    low = (table - high.astype(np.float64)).astype(ml_dtypes.bfloat16)
    return high, low


def z_tables():
    za = np.arange(4)[:, None, None]
    zq = np.arange(4)[None, :, None]
    d = np.arange(ND)[None, None, :]
    z = (16 * d + 4 * zq + za).reshape(4, 512)
    cycle = (np.arange(KZ).astype(np.float32) * np.float32(2.0 * math.pi / KZ)).astype(np.float32)
    phase = (z[:, :, None] * np.arange(HALF)[None, None, :]) % KZ
    kept = np.arange(HALF) <= QK // 2
    cosine = np.where(kept, np.cos(cycle)[phase], 0.0).astype(ml_dtypes.bfloat16)
    sine = np.where(kept, np.sin(cycle)[phase], 0.0).astype(ml_dtypes.bfloat16)
    table = np.concatenate([cosine, sine], 2)
    mirror = np.zeros((2, 256, 128), np.float32)
    lane = np.arange(128)
    mirror[:, 128 - lane, lane] = 1.0
    mirror[1, :, 64] = 0.0
    return table, mirror.astype(ml_dtypes.bfloat16)


def x_tables():
    s = np.arange(ND)
    xa = np.arange(256)
    angle = 2.0 * math.pi * ((xa[:, None] * s[None, :]) % 256) / 256
    real_rows = np.concatenate([np.cos(angle), -np.sin(angle)], 1)
    imag_rows = np.concatenate([np.sin(angle), np.cos(angle)], 1)
    first = np.concatenate(split(np.concatenate([real_rows, imag_rows], 0)), 1)
    m = np.zeros(LANES, np.int64)
    m[: 3 * MODES] = np.arange(3 * MODES) % MODES
    angle = 2.0 * math.pi * (xa[:, None] * m[None, :]) / NX
    twiddle = np.stack([np.cos(angle), np.sin(angle)]).astype(np.float32)
    xb = np.arange(8)
    last = np.zeros((3, 8, 2, LANES))
    for c in range(3):
        angle = 2.0 * math.pi * ((xb[:, None] * np.arange(MODES)[None, :]) % MODES) / MODES
        last[c, :, 0, c * MODES : (c + 1) * MODES] = np.cos(angle)
        last[c, :, 1, c * MODES : (c + 1) * MODES] = -np.sin(angle)
    last = last.reshape(24, 2 * LANES)
    high, low = split(last)
    last = np.concatenate([high, low], 0)
    return first, twiddle, last


def add(p, q):
    return (p[0] + q[0], p[1] + q[1])


def sub(p, q):
    return (p[0] - q[0], p[1] - q[1])


def turn(p):
    return (-p[1], p[0])


def fill(spec, mirror_ref, coef, pair):
    pad = jnp.zeros((LANES - 3 * MODES, 128), jnp.float32)
    for block in range(8):
        turned = []
        for ka in range(4):
            start = ka * QK + (14 - block) * 128
            width = 128 if block == 0 else 256
            matrix = mirror_ref[1 if block == 7 else 0, 0:width, :]
            turned.append(jnp.dot(spec[:, start : start + width], matrix, preferred_element_type=jnp.float32))
        pieces = {}
        for c in range(3):
            near, far = [], []
            for ka in range(4):
                start = ka * QK + block * 128
                x = spec[80 * c : 80 * c + 80, start : start + 128].astype(jnp.float32)
                near.append((x[0:40], x[40:80]))
                far.append((turned[ka][80 * c : 80 * c + 40], turned[ka][80 * c + 40 : 80 * c + 80]))
            sides = []
            for x in (near, far):
                if pair == 0:
                    even, odd = add(x[0], x[2]), add(x[1], x[3])
                else:
                    even, odd = sub(x[0], x[2]), turn(sub(x[1], x[3]))
                sides.append((add(even, odd), sub(even, odd)))
            for zaa in range(2):
                y, r = sides[0][zaa], sides[1][zaa]
                if pair == 1:
                    r = turn(r)
                if zaa == 0:
                    e, o = add(y, r), sub(y, r)
                else:
                    e, o = sub(y, r), add(y, r)
                for name, value in ((0, e[0]), (1, e[1]), (2, -o[1]), (3, o[0])):
                    pieces.setdefault((zaa, name), []).append(value)
        for (zaa, name), values in pieces.items():
            whole = jnp.concatenate(values + [pad], 0)
            top = whole.astype(jnp.bfloat16)
            rows = slice(name % 2 * LANES, (name % 2 + 1) * LANES)
            cols = slice(name // 2 * HALF + block * 128, name // 2 * HALF + (block + 1) * 128)
            coef[pair, zaa, 0, rows, cols] = top
            coef[pair, zaa, 1, rows, cols] = (whole - top.astype(jnp.float32)).astype(jnp.bfloat16)


def plane(tab, coef, wide, msg, pair):
    for zaa in range(2):
        table = tab[pair + 2 * zaa]
        v = lax.dot_general(table, coef[pair, zaa, 0], NT, preferred_element_type=jnp.float32)
        v = v + lax.dot_general(table, coef[pair, zaa, 1], NT, preferred_element_type=jnp.float32)
        for zq in range(4):
            for part in range(2):
                wide[pl.ds(8 * zaa + 2 * zq + part, ND, stride=ROWS), :] = v[
                    zq * ND : (zq + 1) * ND, part * LANES : (part + 1) * LANES
                ]
    msg[pair] = wide[...].astype(jnp.bfloat16).reshape(ND, ROWS, LANES)


def enstrophy(recv, wide, mats, top, rest, first_ref, tw_ref, last_ref, enst, pair):
    scale = 2.0 / math.sqrt(2.0 * KX * KZ)
    wide[...] = recv[pair].reshape(ND * ROWS, LANES).astype(jnp.float32)
    lane = lax.broadcasted_iota(jnp.int32, (ROWS, LANES), 1)
    factor = jnp.where((lane == 0) | (lane == MODES) | (lane == 2 * MODES), 0.5, 1.0)
    wide[0:ROWS, :] = wide[0:ROWS, :] * factor
    for i in range(8):
        cols = slice(i * LANES, (i + 1) * LANES)
        for part in range(2):
            mat = wide[pl.ds(2 * i + part, ND, stride=ROWS), :].astype(jnp.bfloat16)
            mats[part * ND : (part + 1) * ND, cols] = mat
            mats[(part + 2) * ND : (part + 3) * ND, cols] = mat
    cosine, sine = tw_ref[0], tw_ref[1]
    for two in range(4):
        both = mats[:, two * 256 : (two + 1) * 256]
        y = jnp.dot(first_ref[...], both, preferred_element_type=jnp.float32)
        for half in range(2):
            yr = y[0:256, half * LANES : (half + 1) * LANES]
            yi = y[256:512, half * LANES : (half + 1) * LANES]
            t = jnp.concatenate([yr * cosine - yi * sine, yr * sine + yi * cosine], 1)
            high = t.astype(jnp.bfloat16)
            rows = slice((two * 2 + half) * 256, (two * 2 + half + 1) * 256)
            top[rows, :] = high
            rest[rows, :] = (t - high.astype(jnp.float32)).astype(jnp.bfloat16)
    v = lax.dot_general(last_ref[...], top[...], NT, preferred_element_type=jnp.float32)
    v = v[0:24] + v[24:48]
    v = v + lax.dot_general(last_ref[0:24], rest[...], NT, preferred_element_type=jnp.float32)
    v = v * scale
    enst[...] = v[0:8] * v[0:8] + v[8:16] * v[8:16] + v[16:24] * v[16:24]


def zpoint(pair, i):
    return 4 * (i % 4) + 2 * (i // 4) + pair


def spread(row, count):
    tile = jnp.broadcast_to(row, (16, row.shape[1])).astype(jnp.bfloat16)
    return jnp.concatenate([tile] * (count // 16), 0)


def label_sums(me, targets, enst, acc0, acc1, lhs_a, rhs_a, lhs_b, rhs_b, pair):
    upos = (
        lax.broadcasted_iota(jnp.int32, (8, 256), 0) * 256 + lax.broadcasted_iota(jnp.int32, (8, 256), 1)
    ).astype(jnp.float32) / XW - 0.5
    row64 = lax.broadcasted_iota(jnp.int32, (64, 256), 0).astype(jnp.float32).astype(jnp.bfloat16)
    row256 = lax.broadcasted_iota(jnp.int32, (256, 256), 0).astype(jnp.float32).astype(jnp.bfloat16)
    one = jnp.ones((), jnp.bfloat16)
    zero = jnp.zeros((), jnp.bfloat16)

    def build(i, lhs, rhs):
        z = zpoint(pair, i)
        e = enst[:, i * 256 : (i + 1) * 256]
        ehigh = e.astype(jnp.bfloat16).astype(jnp.float32)
        eu = e * upos
        values = [ehigh, e - ehigh, eu, eu * upos]
        for xb in range(8):
            cols = slice(xb * 256, (xb + 1) * 256)
            lab = targets[z : z + 1, cols]
            hit = spread((lab >> 8).astype(jnp.float32), 64) == row64
            lhs[0:64, cols] = jnp.where(hit, one, zero)
            for j, value in enumerate(values):
                lhs[(j + 1) * 64 : (j + 2) * 64, cols] = jnp.where(hit, spread(value[xb : xb + 1], 64), zero)
            near = spread((lab & 255).astype(jnp.float32), 256) == row256
            rhs[:, cols] = jnp.where(near, one, zero)

    def collect(i, lhs, rhs):
        t = lax.dot_general(lhs[...], rhs[...], NT, preferred_element_type=jnp.float32)
        w = (me * ROWS + zpoint(pair, i)).astype(jnp.float32) / ZW - 0.5
        e_sum = t[64:128] + t[128:192]
        eu_sum = t[192:256]
        terms = [t[0:64], e_sum, eu_sum, e_sum * w, t[256:320], eu_sum * w, e_sum * (w * w)]
        for j, term in enumerate(terms):
            acc0[j * 64 : (j + 1) * 64, :] += term[:, :128]
            acc1[j * 64 : (j + 1) * 64, :] += term[:, 128:]

    buffers = ((lhs_a, rhs_a), (lhs_b, rhs_b))
    build(0, *buffers[0])
    for i in range(8):
        if i < 7:
            build(i + 1, *buffers[(i + 1) % 2])
        collect(i, *buffers[i % 2])


def owner_of(core, q):
    return (q // 16 * 2 + core, q % 16)


def kernel(
    spec_hbm, tab_hbm, lab_ref, place_ref, mirror_ref, first_ref, tw_ref, last_ref, out_ref,
    spec, tab, coef, wide, msg, recv, targets, mats, top, rest, enst, acc0, acc1,
    lhs_a, rhs_a, lhs_b, rhs_b, table, mate, part, parts,
    spec_sem, tab_sem, own_sem, plane_send, plane_recv, pair_send, pair_recv, sum_send, sum_recv,
):
    row = lax.axis_index("row")
    col = lax.axis_index("col")
    me = row * 16 + col
    core = row % 2
    mine = row // 2 * 16 + col
    load = pltpu.make_async_copy(spec_hbm, spec, spec_sem)
    load.start()
    order = (0, 2, 1, 3)
    loads = [pltpu.make_async_copy(tab_hbm.at[za], tab.at[za], tab_sem.at[za]) for za in range(4)]
    for za in order:
        loads[za].start()
    barrier = pltpu.get_barrier_semaphore()

    def greet(j, carry):
        d = lax.rem(me + j, ND)
        pl.semaphore_signal(barrier, inc=1, device_id=(d // 16, d % 16), device_id_type=MESH)
        return carry

    lax.fori_loop(1, ND, greet, 0)

    places = jnp.broadcast_to(place_ref[...], (16, LB))
    for i in range(XW // LB):
        cols = slice(i * LB, (i + 1) * LB)
        lab = lab_ref[:, cols]
        targets[:, cols] = jnp.take_along_axis(places, lab >> 7, axis=1) * LB + (lab & 127)
    acc0[...] = jnp.zeros_like(acc0)
    acc1[...] = jnp.zeros_like(acc1)

    load.wait()
    owns = []
    for pair in range(2):
        fill(spec, mirror_ref, coef, pair)
        for zaa in range(2):
            loads[pair + 2 * zaa].wait()
        plane(tab, coef, wide, msg, pair)
        if pair == 0:
            pl.semaphore_wait(barrier, ND - 1)

        def send(j, carry, pair=pair):
            d = lax.rem(me + j, ND)
            pltpu.make_async_remote_copy(
                src_ref=msg.at[pair, d],
                dst_ref=recv.at[pair, me],
                send_sem=plane_send.at[pair],
                recv_sem=plane_recv.at[pair],
                device_id=(d // 16, d % 16),
                device_id_type=MESH,
            ).start()
            return carry

        lax.fori_loop(1, ND, send, 0)
        own = pltpu.make_async_copy(msg.at[pair, me], recv.at[pair, me], own_sem.at[pair])
        own.start()
        owns.append(own)

    for pair in range(2):
        owns[pair].wait()
        others = recv.at[pair, pl.ds(0, ND - 1)]
        pltpu.make_async_copy(others, others, plane_recv.at[pair]).wait()
        enstrophy(recv, wide, mats, top, rest, first_ref, tw_ref, last_ref, enst, pair)
        label_sums(me, targets, enst, acc0, acc1, lhs_a, rhs_a, lhs_b, rhs_b, pair)

    for place in range(NBLK):
        table[place % 2, place % 8 // 2 * 16 + place // 8] = (acc0, acc1)[place % 2][
            pl.ds(place // 2, 8, stride=64), :
        ]
    swap = pltpu.make_async_remote_copy(
        src_ref=table.at[1 - core],
        dst_ref=mate,
        send_sem=pair_send,
        recv_sem=pair_recv,
        device_id=(row + 1 - 2 * core, col),
        device_id_type=MESH,
    )
    swap.start()
    swap.wait()
    part[...] = table[core] + mate[...]

    def send_sum(j, carry):
        q = lax.rem(mine + j, 64)
        pltpu.make_async_remote_copy(
            src_ref=part.at[q],
            dst_ref=parts.at[mine],
            send_sem=sum_send,
            recv_sem=sum_recv,
            device_id=owner_of(core, q),
            device_id_type=MESH,
        ).start()
        return carry

    lax.fori_loop(1, 64, send_sum, 0)
    parts[mine] = part[mine]
    every = parts.at[pl.ds(0, 63)]
    pltpu.make_async_copy(every, every, sum_send).wait()
    pltpu.make_async_copy(every, every, sum_recv).wait()
    for pair in range(2):
        others = msg.at[pair, pl.ds(0, ND - 1)]
        pltpu.make_async_copy(others, others, plane_send.at[pair]).wait()
    out_ref[...] = finish(jnp.sum(parts[...], 0))


def run(spec, table, labels, place, mirror, first, twiddle, last):
    vmem = pl.BlockSpec(memory_space=pltpu.VMEM)
    hbm = pl.BlockSpec(memory_space=pl.ANY)
    f32, bf16 = jnp.float32, jnp.bfloat16
    dma = pltpu.SemaphoreType.DMA
    return pl.pallas_call(
        kernel,
        out_shape=jax.ShapeDtypeStruct((6, 128), f32),
        in_specs=[hbm, hbm] + [vmem] * 6,
        out_specs=vmem,
        scratch_shapes=[
            pltpu.VMEM((6 * MODES, KZ), bf16),
            pltpu.VMEM((4, 512, 2 * HALF), bf16),
            pltpu.VMEM((2, 2, 2, 2 * LANES, 2 * HALF), bf16),
            pltpu.VMEM((ND * ROWS, LANES), f32),
            pltpu.VMEM((2, ND, ROWS, LANES), bf16),
            pltpu.VMEM((2, ND, ROWS, LANES), bf16),
            pltpu.VMEM((ROWS, XW), jnp.int32),
            pltpu.VMEM((512, 8 * LANES), bf16),
            pltpu.VMEM((8 * 256, 2 * LANES), bf16),
            pltpu.VMEM((8 * 256, 2 * LANES), bf16),
            pltpu.VMEM((8, 8 * 256), f32),
            pltpu.VMEM((512, 128), f32),
            pltpu.VMEM((512, 128), f32),
            pltpu.VMEM((320, XW), bf16),
            pltpu.VMEM((256, XW), bf16),
            pltpu.VMEM((320, XW), bf16),
            pltpu.VMEM((256, XW), bf16),
            pltpu.VMEM((2, 64, 8, 128), f32),
            pltpu.VMEM((64, 8, 128), f32),
            pltpu.VMEM((64, 8, 128), f32),
            pltpu.VMEM((64, 8, 128), f32),
            dma, dma((4,)), dma((2,)), dma((2,)), dma((2,)), dma, dma, dma, dma,
        ],
        compiler_params=pltpu.CompilerParams(
            collective_id=0, has_side_effects=True, vmem_limit_bytes=VMEM_LIMIT
        ),
    )(spec, table, labels, place, mirror, first, twiddle, last)


def finish(centred):
    count, s1, u1, w1, uu, uw, ww = (centred[j] for j in range(7))
    s2 = u1 + 0.5 * s1
    s3 = w1 + 0.5 * s1
    s4 = uu + u1 + 0.25 * s1
    s5 = uw + 0.5 * (u1 + w1) + 0.25 * s1
    s6 = ww + w1 + 0.25 * s1
    weight = jnp.maximum(s1, 1.0)
    centre_x = s2 / weight
    centre_z = s3 / weight
    return jnp.stack(
        [
            s1 / jnp.maximum(count, 1.0),
            centre_x,
            centre_z,
            12.0 * (s4 / weight - centre_x * centre_x),
            12.0 * (s5 / weight - centre_x * centre_z),
            12.0 * (s6 / weight - centre_z * centre_z),
        ],
        0,
    )


def solution(mesh):
    table, mirror = z_tables()
    first, twiddle, last = x_tables()

    def on_device(spectral, labels, block_place):
        spec = spectral.reshape(6 * MODES, KZ)
        out = run(spec, table, labels, block_place.reshape(1, NBLK), mirror, first, twiddle, last)
        return out.reshape(6, 1, 128)

    in_specs = (P(None, None, ("row", "col"), None), P(("row", "col"), None), P())
    return jax.shard_map(on_device, mesh=mesh, in_specs=in_specs, out_specs=P(None, "col", "row"), check_vma=False)
```

```python
import math

import jax
import jax.numpy as jnp
import ml_dtypes
import numpy as np
from jax import lax
from jax.experimental import pallas as pl
from jax.experimental.pallas import tpu as pltpu
from jax.sharding import PartitionSpec as P

KX = 5120
KZ = 7680
NX = 10240
ZW = 2048
XW = 2048
ND = 128
MODES = 40
QK = KZ // 4
HALF = 1024
ROWS = 16
LB = 128
NBLK = 128
LANES = 128
MESH = pl.DeviceIdType.MESH
NT = (((1,), (1,)), ((), ()))
VMEM_LIMIT = 60 * 1024 * 1024


def split(table):
    high = table.astype(ml_dtypes.bfloat16)
    low = (table - high.astype(np.float64)).astype(ml_dtypes.bfloat16)
    return high, low


def z_tables():
    za = np.arange(4)[:, None, None]
    zq = np.arange(4)[None, :, None]
    d = np.arange(ND)[None, None, :]
    z = (16 * d + 4 * zq + za).reshape(4, 512)
    cycle = (np.arange(KZ).astype(np.float32) * np.float32(2.0 * math.pi / KZ)).astype(np.float32)
    phase = (z[:, :, None] * np.arange(HALF)[None, None, :]) % KZ
    kept = np.arange(HALF) <= QK // 2
    cosine = np.where(kept, np.cos(cycle)[phase], 0.0).astype(ml_dtypes.bfloat16)
    sine = np.where(kept, np.sin(cycle)[phase], 0.0).astype(ml_dtypes.bfloat16)
    table = np.concatenate([cosine, sine], 2)
    mirror = np.zeros((2, 256, 128), np.float32)
    lane = np.arange(128)
    mirror[:, 128 - lane, lane] = 1.0
    mirror[1, :, 64] = 0.0
    return table, mirror.astype(ml_dtypes.bfloat16)


def x_tables():
    s = np.arange(ND)
    xa = np.arange(256)
    angle = 2.0 * math.pi * ((xa[:, None] * s[None, :]) % 256) / 256
    real_rows = np.concatenate([np.cos(angle), -np.sin(angle)], 1)
    imag_rows = np.concatenate([np.sin(angle), np.cos(angle)], 1)
    first = np.concatenate(split(np.concatenate([real_rows, imag_rows], 0)), 1)
    m = np.zeros(LANES, np.int64)
    m[: 3 * MODES] = np.arange(3 * MODES) % MODES
    angle = 2.0 * math.pi * (xa[:, None] * m[None, :]) / NX
    twiddle = np.stack([np.cos(angle), np.sin(angle)]).astype(np.float32)
    xb = np.arange(8)
    last = np.zeros((3, 8, 2, LANES))
    for c in range(3):
        angle = 2.0 * math.pi * ((xb[:, None] * np.arange(MODES)[None, :]) % MODES) / MODES
        last[c, :, 0, c * MODES : (c + 1) * MODES] = np.cos(angle)
        last[c, :, 1, c * MODES : (c + 1) * MODES] = -np.sin(angle)
    last = last.reshape(24, 2 * LANES)
    high, low = split(last)
    last = np.concatenate([high, low], 0)
    return first, twiddle, last


def add(p, q):
    return (p[0] + q[0], p[1] + q[1])


def sub(p, q):
    return (p[0] - q[0], p[1] - q[1])


def turn(p):
    return (-p[1], p[0])


def fill(spec, mirror_ref, coef, pair):
    pad = jnp.zeros((LANES - 3 * MODES, 128), jnp.float32)
    for block in range(8):
        turned = []
        for ka in range(4):
            start = ka * QK + (14 - block) * 128
            width = 128 if block == 0 else 256
            matrix = mirror_ref[1 if block == 7 else 0, 0:width, :]
            turned.append(jnp.dot(spec[:, start : start + width], matrix, preferred_element_type=jnp.float32))
        pieces = {}
        for c in range(3):
            near, far = [], []
            for ka in range(4):
                start = ka * QK + block * 128
                x = spec[80 * c : 80 * c + 80, start : start + 128].astype(jnp.float32)
                near.append((x[0:40], x[40:80]))
                far.append((turned[ka][80 * c : 80 * c + 40], turned[ka][80 * c + 40 : 80 * c + 80]))
            sides = []
            for x in (near, far):
                if pair == 0:
                    even, odd = add(x[0], x[2]), add(x[1], x[3])
                else:
                    even, odd = sub(x[0], x[2]), turn(sub(x[1], x[3]))
                sides.append((add(even, odd), sub(even, odd)))
            for zaa in range(2):
                y, r = sides[0][zaa], sides[1][zaa]
                if pair == 1:
                    r = turn(r)
                if zaa == 0:
                    e, o = add(y, r), sub(y, r)
                else:
                    e, o = sub(y, r), add(y, r)
                for name, value in ((0, e[0]), (1, e[1]), (2, -o[1]), (3, o[0])):
                    pieces.setdefault((zaa, name), []).append(value)
        for (zaa, name), values in pieces.items():
            whole = jnp.concatenate(values + [pad], 0)
            top = whole.astype(jnp.bfloat16)
            rows = slice(name % 2 * LANES, (name % 2 + 1) * LANES)
            cols = slice(name // 2 * HALF + block * 128, name // 2 * HALF + (block + 1) * 128)
            coef[pair, zaa, 0, rows, cols] = top
            coef[pair, zaa, 1, rows, cols] = (whole - top.astype(jnp.float32)).astype(jnp.bfloat16)


def plane(tab, coef, wide, msg, pair):
    for zaa in range(2):
        table = tab[pair + 2 * zaa]
        v = lax.dot_general(table, coef[pair, zaa, 0], NT, preferred_element_type=jnp.float32)
        v = v + lax.dot_general(table, coef[pair, zaa, 1], NT, preferred_element_type=jnp.float32)
        for zq in range(4):
            for part in range(2):
                wide[pl.ds(8 * zaa + 2 * zq + part, ND, stride=ROWS), :] = v[
                    zq * ND : (zq + 1) * ND, part * LANES : (part + 1) * LANES
                ]
    msg[pair] = wide[...].astype(jnp.bfloat16).reshape(ND, ROWS, LANES)


def enstrophy(recv, wide, mats, top, rest, first_ref, tw_ref, last_ref, enst, pair):
    scale = 2.0 / math.sqrt(2.0 * KX * KZ)
    wide[...] = recv[pair].reshape(ND * ROWS, LANES).astype(jnp.float32)
    lane = lax.broadcasted_iota(jnp.int32, (ROWS, LANES), 1)
    factor = jnp.where((lane == 0) | (lane == MODES) | (lane == 2 * MODES), 0.5, 1.0)
    wide[0:ROWS, :] = wide[0:ROWS, :] * factor
    for i in range(8):
        cols = slice(i * LANES, (i + 1) * LANES)
        for part in range(2):
            mat = wide[pl.ds(2 * i + part, ND, stride=ROWS), :].astype(jnp.bfloat16)
            mats[part * ND : (part + 1) * ND, cols] = mat
            mats[(part + 2) * ND : (part + 3) * ND, cols] = mat
    cosine, sine = tw_ref[0], tw_ref[1]
    for two in range(4):
        both = mats[:, two * 256 : (two + 1) * 256]
        y = jnp.dot(first_ref[...], both, preferred_element_type=jnp.float32)
        for half in range(2):
            yr = y[0:256, half * LANES : (half + 1) * LANES]
            yi = y[256:512, half * LANES : (half + 1) * LANES]
            t = jnp.concatenate([yr * cosine - yi * sine, yr * sine + yi * cosine], 1)
            high = t.astype(jnp.bfloat16)
            rows = slice((two * 2 + half) * 256, (two * 2 + half + 1) * 256)
            top[rows, :] = high
            rest[rows, :] = (t - high.astype(jnp.float32)).astype(jnp.bfloat16)
    v = lax.dot_general(last_ref[...], top[...], NT, preferred_element_type=jnp.float32)
    v = v[0:24] + v[24:48]
    v = v + lax.dot_general(last_ref[0:24], rest[...], NT, preferred_element_type=jnp.float32)
    v = v * scale
    enst[...] = v[0:8] * v[0:8] + v[8:16] * v[8:16] + v[16:24] * v[16:24]


def zpoint(pair, i):
    return 4 * (i % 4) + 2 * (i // 4) + pair


def spread(row, count):
    tile = jnp.broadcast_to(row, (16, row.shape[1])).astype(jnp.bfloat16)
    return jnp.concatenate([tile] * (count // 16), 0)


def label_sums(me, targets, enst, acc0, acc1, lhs_a, rhs_a, lhs_b, rhs_b, pair):
    upos = (
        lax.broadcasted_iota(jnp.int32, (8, 256), 0) * 256 + lax.broadcasted_iota(jnp.int32, (8, 256), 1)
    ).astype(jnp.float32) / XW - 0.5
    row64 = lax.broadcasted_iota(jnp.int32, (64, 256), 0).astype(jnp.float32).astype(jnp.bfloat16)
    row256 = lax.broadcasted_iota(jnp.int32, (256, 256), 0).astype(jnp.float32).astype(jnp.bfloat16)
    one = jnp.ones((), jnp.bfloat16)
    zero = jnp.zeros((), jnp.bfloat16)

    def build(i, lhs, rhs):
        z = zpoint(pair, i)
        e = enst[:, pl.ds(pl.multiple_of(i * 256, 256), 256)]
        ehigh = e.astype(jnp.bfloat16).astype(jnp.float32)
        eu = e * upos
        values = [ehigh, e - ehigh, eu, eu * upos]
        for xb in range(8):
            cols = slice(xb * 256, (xb + 1) * 256)
            lab = targets[pl.ds(z, 1), cols]
            hit = spread((lab >> 8).astype(jnp.float32), 64) == row64
            lhs[0:64, cols] = jnp.where(hit, one, zero)
            for j, value in enumerate(values):
                lhs[(j + 1) * 64 : (j + 2) * 64, cols] = jnp.where(hit, spread(value[xb : xb + 1], 64), zero)
            near = spread((lab & 255).astype(jnp.float32), 256) == row256
            rhs[:, cols] = jnp.where(near, one, zero)

    def collect(i, lhs, rhs):
        t = lax.dot_general(lhs[...], rhs[...], NT, preferred_element_type=jnp.float32)
        w = (me * ROWS + zpoint(pair, i)).astype(jnp.float32) / ZW - 0.5
        e_sum = t[64:128] + t[128:192]
        eu_sum = t[192:256]
        terms = [t[0:64], e_sum, eu_sum, e_sum * w, t[256:320], eu_sum * w, e_sum * (w * w)]
        for j, term in enumerate(terms):
            acc0[j * 64 : (j + 1) * 64, :] += term[:, :128]
            acc1[j * 64 : (j + 1) * 64, :] += term[:, 128:]

    build(0, lhs_a, rhs_a)

    def two_rows(n, carry):
        build(2 * n + 1, lhs_b, rhs_b)
        collect(2 * n, lhs_a, rhs_a)
        build(lax.rem(2 * n + 2, 8), lhs_a, rhs_a)
        collect(2 * n + 1, lhs_b, rhs_b)
        return carry

    lax.fori_loop(0, 4, two_rows, 0)


def owner_of(core, q):
    return (q // 16 * 2 + core, q % 16)


def kernel(
    spec_hbm, tab_hbm, lab_ref, place_ref, mirror_ref, first_ref, tw_ref, last_ref, out_ref,
    spec, tab, coef, wide, msg, recv, targets, mats, top, rest, enst, acc0, acc1,
    lhs_a, rhs_a, lhs_b, rhs_b, table, mate, part, parts,
    spec_sem, tab_sem, own_sem, plane_send, plane_recv, pair_send, pair_recv, sum_send, sum_recv,
):
    row = lax.axis_index("row")
    col = lax.axis_index("col")
    me = row * 16 + col
    core = row % 2
    mine = row // 2 * 16 + col
    load = pltpu.make_async_copy(spec_hbm, spec, spec_sem)
    load.start()
    order = (0, 2, 1, 3)
    loads = [pltpu.make_async_copy(tab_hbm.at[za], tab.at[za], tab_sem.at[za]) for za in range(4)]
    barrier = pltpu.get_barrier_semaphore()

    def greet(j, carry):
        d = lax.rem(me + j, ND)
        pl.semaphore_signal(barrier, inc=1, device_id=(d // 16, d % 16), device_id_type=MESH)
        return carry

    lax.fori_loop(1, ND, greet, 0)

    places = jnp.broadcast_to(place_ref[...], (16, LB))
    for i in range(XW // LB):
        cols = slice(i * LB, (i + 1) * LB)
        lab = lab_ref[:, cols]
        targets[:, cols] = jnp.take_along_axis(places, lab >> 7, axis=1) * LB + (lab & 127)
    acc0[...] = jnp.zeros_like(acc0)
    acc1[...] = jnp.zeros_like(acc1)

    load.wait()
    for za in order:
        loads[za].start()
    owns = []
    for pair in range(2):
        fill(spec, mirror_ref, coef, pair)
        for zaa in range(2):
            loads[pair + 2 * zaa].wait()
        plane(tab, coef, wide, msg, pair)
        if pair == 0:
            pl.semaphore_wait(barrier, ND - 1)

        def send(j, carry, pair=pair):
            d = lax.rem(me + j, ND)
            pltpu.make_async_remote_copy(
                src_ref=msg.at[pair, d],
                dst_ref=recv.at[pair, me],
                send_sem=plane_send.at[pair],
                recv_sem=plane_recv.at[pair],
                device_id=(d // 16, d % 16),
                device_id_type=MESH,
            ).start()
            return carry

        lax.fori_loop(1, ND, send, 0)
        own = pltpu.make_async_copy(msg.at[pair, me], recv.at[pair, me], own_sem.at[pair])
        own.start()
        owns.append(own)

    for pair in range(2):
        owns[pair].wait()
        others = recv.at[pair, pl.ds(0, ND - 1)]
        pltpu.make_async_copy(others, others, plane_recv.at[pair]).wait()
        enstrophy(recv, wide, mats, top, rest, first_ref, tw_ref, last_ref, enst, pair)
        label_sums(me, targets, enst, acc0, acc1, lhs_a, rhs_a, lhs_b, rhs_b, pair)

    for place in range(NBLK):
        table[place % 2, place % 8 // 2 * 16 + place // 8] = (acc0, acc1)[place % 2][
            pl.ds(place // 2, 8, stride=64), :
        ]
    swap = pltpu.make_async_remote_copy(
        src_ref=table.at[1 - core],
        dst_ref=mate,
        send_sem=pair_send,
        recv_sem=pair_recv,
        device_id=(row + 1 - 2 * core, col),
        device_id_type=MESH,
    )
    swap.start()
    swap.wait()
    part[...] = table[core] + mate[...]

    def send_sum(j, carry):
        q = lax.rem(mine + j, 64)
        pltpu.make_async_remote_copy(
            src_ref=part.at[q],
            dst_ref=parts.at[mine],
            send_sem=sum_send,
            recv_sem=sum_recv,
            device_id=owner_of(core, q),
            device_id_type=MESH,
        ).start()
        return carry

    lax.fori_loop(1, 64, send_sum, 0)
    parts[mine] = part[mine]
    every = parts.at[pl.ds(0, 63)]
    pltpu.make_async_copy(every, every, sum_send).wait()
    pltpu.make_async_copy(every, every, sum_recv).wait()
    for pair in range(2):
        others = msg.at[pair, pl.ds(0, ND - 1)]
        pltpu.make_async_copy(others, others, plane_send.at[pair]).wait()
    out_ref[...] = finish(jnp.sum(parts[...], 0))


def run(spec, table, labels, place, mirror, first, twiddle, last):
    vmem = pl.BlockSpec(memory_space=pltpu.VMEM)
    hbm = pl.BlockSpec(memory_space=pl.ANY)
    f32, bf16 = jnp.float32, jnp.bfloat16
    dma = pltpu.SemaphoreType.DMA
    return pl.pallas_call(
        kernel,
        out_shape=jax.ShapeDtypeStruct((6, 128), f32),
        in_specs=[hbm, hbm] + [vmem] * 6,
        out_specs=vmem,
        scratch_shapes=[
            pltpu.VMEM((6 * MODES, KZ), bf16),
            pltpu.VMEM((4, 512, 2 * HALF), bf16),
            pltpu.VMEM((2, 2, 2, 2 * LANES, 2 * HALF), bf16),
            pltpu.VMEM((ND * ROWS, LANES), f32),
            pltpu.VMEM((2, ND, ROWS, LANES), bf16),
            pltpu.VMEM((2, ND, ROWS, LANES), bf16),
            pltpu.VMEM((ROWS, XW), jnp.int32),
            pltpu.VMEM((512, 8 * LANES), bf16),
            pltpu.VMEM((8 * 256, 2 * LANES), bf16),
            pltpu.VMEM((8 * 256, 2 * LANES), bf16),
            pltpu.VMEM((8, 8 * 256), f32),
            pltpu.VMEM((512, 128), f32),
            pltpu.VMEM((512, 128), f32),
            pltpu.VMEM((320, XW), bf16),
            pltpu.VMEM((256, XW), bf16),
            pltpu.VMEM((320, XW), bf16),
            pltpu.VMEM((256, XW), bf16),
            pltpu.VMEM((2, 64, 8, 128), f32),
            pltpu.VMEM((64, 8, 128), f32),
            pltpu.VMEM((64, 8, 128), f32),
            pltpu.VMEM((64, 8, 128), f32),
            dma, dma((4,)), dma((2,)), dma((2,)), dma((2,)), dma, dma, dma, dma,
        ],
        compiler_params=pltpu.CompilerParams(
            collective_id=0, has_side_effects=True, vmem_limit_bytes=VMEM_LIMIT
        ),
    )(spec, table, labels, place, mirror, first, twiddle, last)


def finish(centred):
    count, s1, u1, w1, uu, uw, ww = (centred[j] for j in range(7))
    s2 = u1 + 0.5 * s1
    s3 = w1 + 0.5 * s1
    s4 = uu + u1 + 0.25 * s1
    s5 = uw + 0.5 * (u1 + w1) + 0.25 * s1
    s6 = ww + w1 + 0.25 * s1
    weight = jnp.maximum(s1, 1.0)
    centre_x = s2 / weight
    centre_z = s3 / weight
    return jnp.stack(
        [
            s1 / jnp.maximum(count, 1.0),
            centre_x,
            centre_z,
            12.0 * (s4 / weight - centre_x * centre_x),
            12.0 * (s5 / weight - centre_x * centre_z),
            12.0 * (s6 / weight - centre_z * centre_z),
        ],
        0,
    )


def solution(mesh):
    table, mirror = z_tables()
    first, twiddle, last = x_tables()

    def on_device(spectral, labels, block_place):
        spec = spectral.reshape(6 * MODES, KZ)
        out = run(spec, table, labels, block_place.reshape(1, NBLK), mirror, first, twiddle, last)
        return out.reshape(6, 1, 128)

    in_specs = (P(None, None, ("row", "col"), None), P(("row", "col"), None), P())
    return jax.shard_map(on_device, mesh=mesh, in_specs=in_specs, out_specs=P(None, "col", "row"), check_vma=False)
```

```python
import math

import jax
import jax.numpy as jnp
import ml_dtypes
import numpy as np
from jax import lax
from jax.experimental import pallas as pl
from jax.experimental.pallas import tpu as pltpu
from jax.sharding import PartitionSpec as P

KX = 5120
KZ = 7680
NX = 10240
ZW = 2048
XW = 2048
ND = 128
MODES = 40
QK = KZ // 4
HALF = 1024
ROWS = 16
LB = 128
NBLK = 128
LANES = 128
MESH = pl.DeviceIdType.MESH
NT = (((1,), (1,)), ((), ()))
VMEM_LIMIT = 60 * 1024 * 1024


def split(table):
    high = table.astype(ml_dtypes.bfloat16)
    low = (table - high.astype(np.float64)).astype(ml_dtypes.bfloat16)
    return high, low


def z_tables():
    za = np.arange(4)[:, None, None]
    zq = np.arange(4)[None, :, None]
    d = np.arange(ND)[None, None, :]
    z = (16 * d + 4 * zq + za).reshape(4, 512)
    cycle = (np.arange(KZ).astype(np.float32) * np.float32(2.0 * math.pi / KZ)).astype(np.float32)
    phase = (z[:, :, None] * np.arange(HALF)[None, None, :]) % KZ
    kept = np.arange(HALF) <= QK // 2
    cosine = np.where(kept, np.cos(cycle)[phase], 0.0).astype(ml_dtypes.bfloat16)
    sine = np.where(kept, np.sin(cycle)[phase], 0.0).astype(ml_dtypes.bfloat16)
    table = np.concatenate([cosine, sine], 2)
    mirror = np.zeros((2, 256, 128), np.float32)
    lane = np.arange(128)
    mirror[:, 128 - lane, lane] = 1.0
    mirror[1, :, 64] = 0.0
    return table, mirror.astype(ml_dtypes.bfloat16)


def x_tables():
    s = np.arange(ND)
    xa = np.arange(256)
    angle = 2.0 * math.pi * ((xa[:, None] * s[None, :]) % 256) / 256
    real_rows = np.concatenate([np.cos(angle), -np.sin(angle)], 1)
    imag_rows = np.concatenate([np.sin(angle), np.cos(angle)], 1)
    first = np.concatenate(split(np.concatenate([real_rows, imag_rows], 0)), 1)
    m = np.zeros(LANES, np.int64)
    m[: 3 * MODES] = np.arange(3 * MODES) % MODES
    angle = 2.0 * math.pi * (xa[:, None] * m[None, :]) / NX
    twiddle = np.stack([np.cos(angle), np.sin(angle)]).astype(np.float32)
    xb = np.arange(8)
    last = np.zeros((3, 8, 2, LANES))
    for c in range(3):
        angle = 2.0 * math.pi * ((xb[:, None] * np.arange(MODES)[None, :]) % MODES) / MODES
        last[c, :, 0, c * MODES : (c + 1) * MODES] = np.cos(angle)
        last[c, :, 1, c * MODES : (c + 1) * MODES] = -np.sin(angle)
    last = last.reshape(24, 2 * LANES)
    high, low = split(last)
    last = np.concatenate([high, low], 0)
    return first, twiddle, last


def add(p, q):
    return (p[0] + q[0], p[1] + q[1])


def sub(p, q):
    return (p[0] - q[0], p[1] - q[1])


def turn(p):
    return (-p[1], p[0])


def fill(spec, mirror_ref, coef, pair):
    pad = jnp.zeros((LANES - 3 * MODES, 128), jnp.float32)
    for block in range(8):
        turned = []
        for ka in range(4):
            start = ka * QK + (14 - block) * 128
            width = 128 if block == 0 else 256
            matrix = mirror_ref[1 if block == 7 else 0, 0:width, :]
            turned.append(jnp.dot(spec[:, start : start + width], matrix, preferred_element_type=jnp.float32))
        pieces = {}
        for c in range(3):
            near, far = [], []
            for ka in range(4):
                start = ka * QK + block * 128
                x = spec[80 * c : 80 * c + 80, start : start + 128].astype(jnp.float32)
                near.append((x[0:40], x[40:80]))
                far.append((turned[ka][80 * c : 80 * c + 40], turned[ka][80 * c + 40 : 80 * c + 80]))
            sides = []
            for x in (near, far):
                if pair == 0:
                    even, odd = add(x[0], x[2]), add(x[1], x[3])
                else:
                    even, odd = sub(x[0], x[2]), turn(sub(x[1], x[3]))
                sides.append((add(even, odd), sub(even, odd)))
            for zaa in range(2):
                y, r = sides[0][zaa], sides[1][zaa]
                if pair == 1:
                    r = turn(r)
                if zaa == 0:
                    e, o = add(y, r), sub(y, r)
                else:
                    e, o = sub(y, r), add(y, r)
                for name, value in ((0, e[0]), (1, e[1]), (2, -o[1]), (3, o[0])):
                    pieces.setdefault((zaa, name), []).append(value)
        for (zaa, name), values in pieces.items():
            whole = jnp.concatenate(values + [pad], 0)
            top = whole.astype(jnp.bfloat16)
            rows = slice(name % 2 * LANES, (name % 2 + 1) * LANES)
            cols = slice(name // 2 * HALF + block * 128, name // 2 * HALF + (block + 1) * 128)
            coef[pair, zaa, 0, rows, cols] = top
            coef[pair, zaa, 1, rows, cols] = (whole - top.astype(jnp.float32)).astype(jnp.bfloat16)


def plane(tab, coef, wide, msg, pair):
    for zaa in range(2):
        table = tab[pair + 2 * zaa]
        v = lax.dot_general(table, coef[pair, zaa, 0], NT, preferred_element_type=jnp.float32)
        v = v + lax.dot_general(table, coef[pair, zaa, 1], NT, preferred_element_type=jnp.float32)
        for zq in range(4):
            for part in range(2):
                wide[pl.ds(8 * zaa + 2 * zq + part, ND, stride=ROWS), :] = v[
                    zq * ND : (zq + 1) * ND, part * LANES : (part + 1) * LANES
                ]
    msg[pair] = wide[...].astype(jnp.bfloat16).reshape(ND, ROWS, LANES)


def enstrophy(recv, wide, mats, top, rest, first_ref, tw_ref, last_ref, enst, pair):
    scale = 2.0 / math.sqrt(2.0 * KX * KZ)
    wide[...] = recv[pair].reshape(ND * ROWS, LANES).astype(jnp.float32)
    lane = lax.broadcasted_iota(jnp.int32, (ROWS, LANES), 1)
    factor = jnp.where((lane == 0) | (lane == MODES) | (lane == 2 * MODES), 0.5, 1.0)
    wide[0:ROWS, :] = wide[0:ROWS, :] * factor
    for i in range(8):
        cols = slice(i * LANES, (i + 1) * LANES)
        for part in range(2):
            mat = wide[pl.ds(2 * i + part, ND, stride=ROWS), :].astype(jnp.bfloat16)
            mats[part * ND : (part + 1) * ND, cols] = mat
            mats[(part + 2) * ND : (part + 3) * ND, cols] = mat
    cosine, sine = tw_ref[0], tw_ref[1]
    for two in range(4):
        both = mats[:, two * 256 : (two + 1) * 256]
        y = jnp.dot(first_ref[...], both, preferred_element_type=jnp.float32)
        for half in range(2):
            yr = y[0:256, half * LANES : (half + 1) * LANES]
            yi = y[256:512, half * LANES : (half + 1) * LANES]
            t = jnp.concatenate([yr * cosine - yi * sine, yr * sine + yi * cosine], 1)
            high = t.astype(jnp.bfloat16)
            rows = slice((two * 2 + half) * 256, (two * 2 + half + 1) * 256)
            top[rows, :] = high
            rest[rows, :] = (t - high.astype(jnp.float32)).astype(jnp.bfloat16)
    v = lax.dot_general(last_ref[...], top[...], NT, preferred_element_type=jnp.float32)
    v = v[0:24] + v[24:48]
    v = v + lax.dot_general(last_ref[0:24], rest[...], NT, preferred_element_type=jnp.float32)
    v = v * scale
    enst[...] = v[0:8] * v[0:8] + v[8:16] * v[8:16] + v[16:24] * v[16:24]


def zpoint(pair, i):
    return 4 * (i % 4) + 2 * (i // 4) + pair


def spread(row, count):
    tile = jnp.broadcast_to(row, (16, row.shape[1])).astype(jnp.bfloat16)
    return jnp.concatenate([tile] * (count // 16), 0)


def label_sums(me, targets, enst, acc0, acc1, lhs_a, rhs_a, lhs_b, rhs_b, pair):
    upos = (
        lax.broadcasted_iota(jnp.int32, (8, 256), 0) * 256 + lax.broadcasted_iota(jnp.int32, (8, 256), 1)
    ).astype(jnp.float32) / XW - 0.5
    row64 = lax.broadcasted_iota(jnp.int32, (64, 256), 0).astype(jnp.float32).astype(jnp.bfloat16)
    row256 = lax.broadcasted_iota(jnp.int32, (256, 256), 0).astype(jnp.float32).astype(jnp.bfloat16)
    one = jnp.ones((), jnp.bfloat16)
    zero = jnp.zeros((), jnp.bfloat16)

    def build(i, lhs, rhs):
        z = zpoint(pair, i)
        e = enst[:, pl.ds(pl.multiple_of(i * 256, 256), 256)]
        ehigh = e.astype(jnp.bfloat16).astype(jnp.float32)
        eu = e * upos
        values = [ehigh, e - ehigh, eu, eu * upos]
        for xb in range(8):
            cols = slice(xb * 256, (xb + 1) * 256)
            lab = targets[pl.ds(z, 1), cols]
            hit = spread((lab >> 8).astype(jnp.float32), 64) == row64
            lhs[0:64, cols] = jnp.where(hit, one, zero)
            for j, value in enumerate(values):
                lhs[(j + 1) * 64 : (j + 2) * 64, cols] = jnp.where(hit, spread(value[xb : xb + 1], 64), zero)
            near = spread((lab & 255).astype(jnp.float32), 256) == row256
            rhs[:, cols] = jnp.where(near, one, zero)

    def collect(i, lhs, rhs):
        t = lax.dot_general(lhs[...], rhs[...], NT, preferred_element_type=jnp.float32)
        w = (me * ROWS + zpoint(pair, i)).astype(jnp.float32) / ZW - 0.5
        e_sum = t[64:128] + t[128:192]
        eu_sum = t[192:256]
        terms = [t[0:64], e_sum, eu_sum, e_sum * w, t[256:320], eu_sum * w, e_sum * (w * w)]
        for j, term in enumerate(terms):
            acc0[j * 64 : (j + 1) * 64, :] += term[:, :128]
            acc1[j * 64 : (j + 1) * 64, :] += term[:, 128:]

    buffers = ((lhs_a, rhs_a), (lhs_b, rhs_b))
    build(0, lhs_a, rhs_a)

    def four_rows(n, carry):
        for k in range(4):
            build(4 * n + k + 1 if k < 3 else lax.rem(4 * n + 4, 8), *buffers[(k + 1) % 2])
            collect(4 * n + k, *buffers[k % 2])
        return carry

    lax.fori_loop(0, 2, four_rows, 0)


def owner_of(core, q):
    return (q // 16 * 2 + core, q % 16)


def kernel(
    spec_hbm, tab_hbm, lab_ref, place_ref, mirror_ref, first_ref, tw_ref, last_ref, out_ref,
    spec, tab, coef, wide, msg, recv, targets, mats, top, rest, enst, acc0, acc1,
    lhs_a, rhs_a, lhs_b, rhs_b, table, mate, part, parts,
    spec_sem, tab_sem, own_sem, plane_send, plane_recv, pair_send, pair_recv, sum_send, sum_recv,
):
    row = lax.axis_index("row")
    col = lax.axis_index("col")
    me = row * 16 + col
    core = row % 2
    mine = row // 2 * 16 + col
    load = pltpu.make_async_copy(spec_hbm, spec, spec_sem)
    load.start()
    order = (0, 2, 1, 3)
    loads = [pltpu.make_async_copy(tab_hbm.at[za], tab.at[za], tab_sem.at[za]) for za in range(4)]
    barrier = pltpu.get_barrier_semaphore()

    def greet(j, carry):
        d = lax.rem(me + j, ND)
        pl.semaphore_signal(barrier, inc=1, device_id=(d // 16, d % 16), device_id_type=MESH)
        return carry

    lax.fori_loop(1, ND, greet, 0)

    places = jnp.broadcast_to(place_ref[...], (16, LB))
    for i in range(XW // LB):
        cols = slice(i * LB, (i + 1) * LB)
        lab = lab_ref[:, cols]
        targets[:, cols] = jnp.take_along_axis(places, lab >> 7, axis=1) * LB + (lab & 127)
    acc0[...] = jnp.zeros_like(acc0)
    acc1[...] = jnp.zeros_like(acc1)

    load.wait()
    for za in order:
        loads[za].start()
    owns = []
    for pair in range(2):
        fill(spec, mirror_ref, coef, pair)
        for zaa in range(2):
            loads[pair + 2 * zaa].wait()
        plane(tab, coef, wide, msg, pair)
        if pair == 0:
            pl.semaphore_wait(barrier, ND - 1)

        def send(j, carry, pair=pair):
            d = lax.rem(me + j, ND)
            pltpu.make_async_remote_copy(
                src_ref=msg.at[pair, d],
                dst_ref=recv.at[pair, me],
                send_sem=plane_send.at[pair],
                recv_sem=plane_recv.at[pair],
                device_id=(d // 16, d % 16),
                device_id_type=MESH,
            ).start()
            return carry

        lax.fori_loop(1, ND, send, 0)
        own = pltpu.make_async_copy(msg.at[pair, me], recv.at[pair, me], own_sem.at[pair])
        own.start()
        owns.append(own)

    for pair in range(2):
        owns[pair].wait()
        others = recv.at[pair, pl.ds(0, ND - 1)]
        pltpu.make_async_copy(others, others, plane_recv.at[pair]).wait()
        enstrophy(recv, wide, mats, top, rest, first_ref, tw_ref, last_ref, enst, pair)
        label_sums(me, targets, enst, acc0, acc1, lhs_a, rhs_a, lhs_b, rhs_b, pair)

    for place in range(NBLK):
        table[place % 2, place % 8 // 2 * 16 + place // 8] = (acc0, acc1)[place % 2][
            pl.ds(place // 2, 8, stride=64), :
        ]
    swap = pltpu.make_async_remote_copy(
        src_ref=table.at[1 - core],
        dst_ref=mate,
        send_sem=pair_send,
        recv_sem=pair_recv,
        device_id=(row + 1 - 2 * core, col),
        device_id_type=MESH,
    )
    swap.start()
    swap.wait()
    part[...] = table[core] + mate[...]

    def send_sum(j, carry):
        q = lax.rem(mine + j, 64)
        pltpu.make_async_remote_copy(
            src_ref=part.at[q],
            dst_ref=parts.at[mine],
            send_sem=sum_send,
            recv_sem=sum_recv,
            device_id=owner_of(core, q),
            device_id_type=MESH,
        ).start()
        return carry

    lax.fori_loop(1, 64, send_sum, 0)
    parts[mine] = part[mine]
    every = parts.at[pl.ds(0, 63)]
    pltpu.make_async_copy(every, every, sum_send).wait()
    pltpu.make_async_copy(every, every, sum_recv).wait()
    for pair in range(2):
        others = msg.at[pair, pl.ds(0, ND - 1)]
        pltpu.make_async_copy(others, others, plane_send.at[pair]).wait()
    out_ref[...] = finish(jnp.sum(parts[...], 0))


def run(spec, table, labels, place, mirror, first, twiddle, last):
    vmem = pl.BlockSpec(memory_space=pltpu.VMEM)
    hbm = pl.BlockSpec(memory_space=pl.ANY)
    f32, bf16 = jnp.float32, jnp.bfloat16
    dma = pltpu.SemaphoreType.DMA
    return pl.pallas_call(
        kernel,
        out_shape=pltpu.VMEM((6, 128), f32),
        in_specs=[hbm, hbm] + [vmem] * 6,
        out_specs=vmem,
        scratch_shapes=[
            pltpu.VMEM((6 * MODES, KZ), bf16),
            pltpu.VMEM((4, 512, 2 * HALF), bf16),
            pltpu.VMEM((2, 2, 2, 2 * LANES, 2 * HALF), bf16),
            pltpu.VMEM((ND * ROWS, LANES), f32),
            pltpu.VMEM((2, ND, ROWS, LANES), bf16),
            pltpu.VMEM((2, ND, ROWS, LANES), bf16),
            pltpu.VMEM((ROWS, XW), jnp.int32),
            pltpu.VMEM((512, 8 * LANES), bf16),
            pltpu.VMEM((8 * 256, 2 * LANES), bf16),
            pltpu.VMEM((8 * 256, 2 * LANES), bf16),
            pltpu.VMEM((8, 8 * 256), f32),
            pltpu.VMEM((512, 128), f32),
            pltpu.VMEM((512, 128), f32),
            pltpu.VMEM((320, XW), bf16),
            pltpu.VMEM((256, XW), bf16),
            pltpu.VMEM((320, XW), bf16),
            pltpu.VMEM((256, XW), bf16),
            pltpu.VMEM((2, 64, 8, 128), f32),
            pltpu.VMEM((64, 8, 128), f32),
            pltpu.VMEM((64, 8, 128), f32),
            pltpu.VMEM((64, 8, 128), f32),
            dma, dma((4,)), dma((2,)), dma((2,)), dma((2,)), dma, dma, dma, dma,
        ],
        compiler_params=pltpu.CompilerParams(
            collective_id=0, has_side_effects=True, vmem_limit_bytes=VMEM_LIMIT
        ),
    )(spec, table, labels, place, mirror, first, twiddle, last)


def finish(centred):
    count, s1, u1, w1, uu, uw, ww = (centred[j] for j in range(7))
    s2 = u1 + 0.5 * s1
    s3 = w1 + 0.5 * s1
    s4 = uu + u1 + 0.25 * s1
    s5 = uw + 0.5 * (u1 + w1) + 0.25 * s1
    s6 = ww + w1 + 0.25 * s1
    weight = jnp.maximum(s1, 1.0)
    centre_x = s2 / weight
    centre_z = s3 / weight
    return jnp.stack(
        [
            s1 / jnp.maximum(count, 1.0),
            centre_x,
            centre_z,
            12.0 * (s4 / weight - centre_x * centre_x),
            12.0 * (s5 / weight - centre_x * centre_z),
            12.0 * (s6 / weight - centre_z * centre_z),
        ],
        0,
    )


def solution(mesh):
    table, mirror = z_tables()
    first, twiddle, last = x_tables()

    def on_device(spectral, labels, block_place):
        spec = spectral.reshape(6 * MODES, KZ)
        out = run(spec, table, labels, block_place.reshape(1, NBLK), mirror, first, twiddle, last)
        return out.reshape(6, 1, 128)

    in_specs = (P(None, None, ("row", "col"), None), P(("row", "col"), None), P())
    return jax.shard_map(on_device, mesh=mesh, in_specs=in_specs, out_specs=P(None, "col", "row"), check_vma=False)
```

```python
import math

import jax
import jax.numpy as jnp
import ml_dtypes
import numpy as np
from jax import lax
from jax.experimental import pallas as pl
from jax.experimental.pallas import tpu as pltpu
from jax.sharding import PartitionSpec as P

KX = 5120
KZ = 7680
NX = 10240
ZW = 2048
XW = 2048
ND = 128
MODES = 40
QK = KZ // 4
HALF = 1024
ROWS = 16
LB = 128
NBLK = 128
LANES = 128
MESH = pl.DeviceIdType.MESH
NT = (((1,), (1,)), ((), ()))
VMEM_LIMIT = 60 * 1024 * 1024


def split(table):
    high = table.astype(ml_dtypes.bfloat16)
    low = (table - high.astype(np.float64)).astype(ml_dtypes.bfloat16)
    return high, low


def z_tables():
    za = np.arange(4)[:, None, None]
    zq = np.arange(4)[None, :, None]
    d = np.arange(ND)[None, None, :]
    z = (16 * d + 4 * zq + za).reshape(4, 512)
    cycle = (np.arange(KZ).astype(np.float32) * np.float32(2.0 * math.pi / KZ)).astype(np.float32)
    phase = (z[:, :, None] * np.arange(HALF)[None, None, :]) % KZ
    kept = np.arange(HALF) <= QK // 2
    cosine = np.where(kept, np.cos(cycle)[phase], 0.0).astype(ml_dtypes.bfloat16)
    sine = np.where(kept, np.sin(cycle)[phase], 0.0).astype(ml_dtypes.bfloat16)
    table = np.concatenate([cosine, sine], 2)
    mirror = np.zeros((2, 256, 128), np.float32)
    lane = np.arange(128)
    mirror[:, 128 - lane, lane] = 1.0
    mirror[1, :, 64] = 0.0
    return table, mirror.astype(ml_dtypes.bfloat16)


def x_tables():
    s = np.arange(ND)
    xa = np.arange(256)
    angle = 2.0 * math.pi * ((xa[:, None] * s[None, :]) % 256) / 256
    real_rows = np.concatenate([np.cos(angle), -np.sin(angle)], 1)
    imag_rows = np.concatenate([np.sin(angle), np.cos(angle)], 1)
    first = np.concatenate(split(np.concatenate([real_rows, imag_rows], 0)), 1)
    m = np.zeros(LANES, np.int64)
    m[: 3 * MODES] = np.arange(3 * MODES) % MODES
    angle = 2.0 * math.pi * (xa[:, None] * m[None, :]) / NX
    twiddle = np.stack([np.cos(angle), np.sin(angle)]).astype(np.float32)
    xb = np.arange(8)
    last = np.zeros((3, 8, 2, LANES))
    for c in range(3):
        angle = 2.0 * math.pi * ((xb[:, None] * np.arange(MODES)[None, :]) % MODES) / MODES
        last[c, :, 0, c * MODES : (c + 1) * MODES] = np.cos(angle)
        last[c, :, 1, c * MODES : (c + 1) * MODES] = -np.sin(angle)
    last = last.reshape(24, 2 * LANES)
    high, low = split(last)
    last = np.concatenate([high, low], 0)
    return first, twiddle, last


def add(p, q):
    return (p[0] + q[0], p[1] + q[1])


def sub(p, q):
    return (p[0] - q[0], p[1] - q[1])


def turn(p):
    return (-p[1], p[0])


def fill(spec, mirror_ref, coef, pair):
    pad = jnp.zeros((LANES - 3 * MODES, 128), jnp.float32)
    for block in range(8):
        turned = []
        for ka in range(4):
            start = ka * QK + (14 - block) * 128
            width = 128 if block == 0 else 256
            matrix = mirror_ref[1 if block == 7 else 0, 0:width, :]
            turned.append(jnp.dot(spec[:, start : start + width], matrix, preferred_element_type=jnp.float32))
        pieces = {}
        for c in range(3):
            near, far = [], []
            for ka in range(4):
                start = ka * QK + block * 128
                x = spec[80 * c : 80 * c + 80, start : start + 128].astype(jnp.float32)
                near.append((x[0:40], x[40:80]))
                far.append((turned[ka][80 * c : 80 * c + 40], turned[ka][80 * c + 40 : 80 * c + 80]))
            sides = []
            for x in (near, far):
                if pair == 0:
                    even, odd = add(x[0], x[2]), add(x[1], x[3])
                else:
                    even, odd = sub(x[0], x[2]), turn(sub(x[1], x[3]))
                sides.append((add(even, odd), sub(even, odd)))
            for zaa in range(2):
                y, r = sides[0][zaa], sides[1][zaa]
                if pair == 1:
                    r = turn(r)
                if zaa == 0:
                    e, o = add(y, r), sub(y, r)
                else:
                    e, o = sub(y, r), add(y, r)
                for name, value in ((0, e[0]), (1, e[1]), (2, -o[1]), (3, o[0])):
                    pieces.setdefault((zaa, name), []).append(value)
        for (zaa, name), values in pieces.items():
            whole = jnp.concatenate(values + [pad], 0)
            rows = slice(name % 2 * LANES, (name % 2 + 1) * LANES)
            cols = slice(name // 2 * HALF + block * 128, name // 2 * HALF + (block + 1) * 128)
            coef[pair, zaa, rows, cols] = whole.astype(jnp.bfloat16)


def plane(tab, coef, wide, msg, pair):
    for zaa in range(2):
        table = tab[pair + 2 * zaa]
        v = lax.dot_general(table, coef[pair, zaa], NT, preferred_element_type=jnp.float32)
        for zq in range(4):
            for part in range(2):
                wide[pl.ds(8 * zaa + 2 * zq + part, ND, stride=ROWS), :] = v[
                    zq * ND : (zq + 1) * ND, part * LANES : (part + 1) * LANES
                ]
    msg[pair] = wide[...].astype(jnp.bfloat16).reshape(ND, ROWS, LANES)


def enstrophy(recv, wide, mats, top, rest, first_ref, tw_ref, last_ref, enst, pair):
    scale = 2.0 / math.sqrt(2.0 * KX * KZ)
    wide[...] = recv[pair].reshape(ND * ROWS, LANES).astype(jnp.float32)
    lane = lax.broadcasted_iota(jnp.int32, (ROWS, LANES), 1)
    factor = jnp.where((lane == 0) | (lane == MODES) | (lane == 2 * MODES), 0.5, 1.0)
    wide[0:ROWS, :] = wide[0:ROWS, :] * factor
    for i in range(8):
        cols = slice(i * LANES, (i + 1) * LANES)
        for part in range(2):
            mat = wide[pl.ds(2 * i + part, ND, stride=ROWS), :].astype(jnp.bfloat16)
            mats[part * ND : (part + 1) * ND, cols] = mat
            mats[(part + 2) * ND : (part + 3) * ND, cols] = mat
    cosine, sine = tw_ref[0], tw_ref[1]
    for two in range(4):
        both = mats[:, two * 256 : (two + 1) * 256]
        y = jnp.dot(first_ref[...], both, preferred_element_type=jnp.float32)
        for half in range(2):
            yr = y[0:256, half * LANES : (half + 1) * LANES]
            yi = y[256:512, half * LANES : (half + 1) * LANES]
            t = jnp.concatenate([yr * cosine - yi * sine, yr * sine + yi * cosine], 1)
            high = t.astype(jnp.bfloat16)
            rows = slice((two * 2 + half) * 256, (two * 2 + half + 1) * 256)
            top[rows, :] = high
            rest[rows, :] = (t - high.astype(jnp.float32)).astype(jnp.bfloat16)
    v = lax.dot_general(last_ref[...], top[...], NT, preferred_element_type=jnp.float32)
    v = v[0:24] + v[24:48]
    v = v + lax.dot_general(last_ref[0:24], rest[...], NT, preferred_element_type=jnp.float32)
    v = v * scale
    enst[...] = v[0:8] * v[0:8] + v[8:16] * v[8:16] + v[16:24] * v[16:24]


def zpoint(pair, i):
    return 4 * (i % 4) + 2 * (i // 4) + pair


def spread(row, count):
    tile = jnp.broadcast_to(row, (16, row.shape[1])).astype(jnp.bfloat16)
    return jnp.concatenate([tile] * (count // 16), 0)


def label_sums(me, targets, enst, acc0, acc1, lhs_a, rhs_a, lhs_b, rhs_b, pair):
    upos = (
        lax.broadcasted_iota(jnp.int32, (8, 256), 0) * 256 + lax.broadcasted_iota(jnp.int32, (8, 256), 1)
    ).astype(jnp.float32) / XW - 0.5
    row64 = lax.broadcasted_iota(jnp.int32, (64, 256), 0).astype(jnp.float32).astype(jnp.bfloat16)
    row256 = lax.broadcasted_iota(jnp.int32, (256, 256), 0).astype(jnp.float32).astype(jnp.bfloat16)
    one = jnp.ones((), jnp.bfloat16)
    zero = jnp.zeros((), jnp.bfloat16)

    def build(i, lhs, rhs):
        z = zpoint(pair, i)
        e = enst[:, pl.ds(pl.multiple_of(i * 256, 256), 256)]
        ehigh = e.astype(jnp.bfloat16).astype(jnp.float32)
        eu = e * upos
        values = [ehigh, e - ehigh, eu, eu * upos]
        for xb in range(8):
            cols = slice(xb * 256, (xb + 1) * 256)
            lab = targets[pl.ds(z, 1), cols]
            hit = spread((lab >> 8).astype(jnp.float32), 64) == row64
            lhs[0:64, cols] = jnp.where(hit, one, zero)
            for j, value in enumerate(values):
                lhs[(j + 1) * 64 : (j + 2) * 64, cols] = jnp.where(hit, spread(value[xb : xb + 1], 64), zero)
            near = spread((lab & 255).astype(jnp.float32), 256) == row256
            rhs[:, cols] = jnp.where(near, one, zero)

    def collect(i, lhs, rhs):
        t = lax.dot_general(lhs[...], rhs[...], NT, preferred_element_type=jnp.float32)
        w = (me * ROWS + zpoint(pair, i)).astype(jnp.float32) / ZW - 0.5
        e_sum = t[64:128] + t[128:192]
        eu_sum = t[192:256]
        terms = [t[0:64], e_sum, eu_sum, e_sum * w, t[256:320], eu_sum * w, e_sum * (w * w)]
        for j, term in enumerate(terms):
            acc0[j * 64 : (j + 1) * 64, :] += term[:, :128]
            acc1[j * 64 : (j + 1) * 64, :] += term[:, 128:]

    buffers = ((lhs_a, rhs_a), (lhs_b, rhs_b))
    build(0, lhs_a, rhs_a)

    def four_rows(n, carry):
        for k in range(4):
            build(4 * n + k + 1 if k < 3 else lax.rem(4 * n + 4, 8), *buffers[(k + 1) % 2])
            collect(4 * n + k, *buffers[k % 2])
        return carry

    lax.fori_loop(0, 2, four_rows, 0)


def owner_of(core, q):
    return (q // 16 * 2 + core, q % 16)


def kernel(
    spec_hbm, tab_hbm, lab_ref, place_ref, mirror_ref, first_ref, tw_ref, last_ref, out_ref,
    spec, tab, coef, wide, msg, recv, targets, mats, top, rest, enst, acc,
    lhs_a, rhs_a, lhs_b, rhs_b, table, mate, part, parts,
    spec_sem, tab_sem, own_sem, plane_send, plane_recv, pair_send, pair_recv, sum_send, sum_recv,
):
    row = lax.axis_index("row")
    col = lax.axis_index("col")
    me = row * 16 + col
    core = row % 2
    mine = row // 2 * 16 + col
    load = pltpu.make_async_copy(spec_hbm, spec, spec_sem)
    load.start()
    order = (0, 2, 1, 3)
    loads = [pltpu.make_async_copy(tab_hbm.at[za], tab.at[za], tab_sem.at[za]) for za in range(4)]
    barrier = pltpu.get_barrier_semaphore()

    def greet(j, carry):
        d = lax.rem(me + j, ND)
        pl.semaphore_signal(barrier, inc=1, device_id=(d // 16, d % 16), device_id_type=MESH)
        return carry

    lax.fori_loop(1, ND, greet, 0)

    places = jnp.broadcast_to(place_ref[...], (16, LB))
    for i in range(XW // LB):
        cols = slice(i * LB, (i + 1) * LB)
        lab = lab_ref[:, cols]
        targets[:, cols] = jnp.take_along_axis(places, lab >> 7, axis=1) * LB + (lab & 127)
    acc[...] = jnp.zeros_like(acc)

    load.wait()
    for za in order:
        loads[za].start()
    owns = []
    for pair in range(2):
        fill(spec, mirror_ref, coef, pair)
        for zaa in range(2):
            loads[pair + 2 * zaa].wait()
        plane(tab, coef, wide, msg, pair)
        if pair == 0:
            pl.semaphore_wait(barrier, ND - 1)

        def send(j, carry, pair=pair):
            d = lax.rem(me + j, ND)
            pltpu.make_async_remote_copy(
                src_ref=msg.at[pair, d],
                dst_ref=recv.at[pair, me],
                send_sem=plane_send.at[pair],
                recv_sem=plane_recv.at[pair],
                device_id=(d // 16, d % 16),
                device_id_type=MESH,
            ).start()
            return carry

        lax.fori_loop(1, ND, send, 0)
        own = pltpu.make_async_copy(msg.at[pair, me], recv.at[pair, me], own_sem.at[pair])
        own.start()
        owns.append(own)

    for pair in range(2):
        owns[pair].wait()
        others = recv.at[pair, pl.ds(0, ND - 1)]
        pltpu.make_async_copy(others, others, plane_recv.at[pair]).wait()
        enstrophy(recv, wide, mats, top, rest, first_ref, tw_ref, last_ref, enst, pair)
        label_sums(me, targets, enst, acc.at[0], acc.at[1], lhs_a, rhs_a, lhs_b, rhs_b, pair)

    def hand_out(half):
        for n in range(64):
            table[half, n % 4 * 16 + n // 4] = acc[half, pl.ds(n, 8, stride=64), :]

    hand_out(1 - core)
    swap = pltpu.make_async_remote_copy(
        src_ref=table.at[1 - core],
        dst_ref=mate,
        send_sem=pair_send,
        recv_sem=pair_recv,
        device_id=(row + 1 - 2 * core, col),
        device_id_type=MESH,
    )
    swap.start()
    hand_out(core)
    swap.wait()
    part[...] = table[core] + mate[...]

    def send_sum(j, carry):
        q = lax.rem(mine + j, 64)
        pltpu.make_async_remote_copy(
            src_ref=part.at[q],
            dst_ref=parts.at[mine],
            send_sem=sum_send,
            recv_sem=sum_recv,
            device_id=owner_of(core, q),
            device_id_type=MESH,
        ).start()
        return carry

    lax.fori_loop(1, 64, send_sum, 0)
    parts[mine] = part[mine]
    every = parts.at[pl.ds(0, 63)]
    pltpu.make_async_copy(every, every, sum_send).wait()
    pltpu.make_async_copy(every, every, sum_recv).wait()
    for pair in range(2):
        others = msg.at[pair, pl.ds(0, ND - 1)]
        pltpu.make_async_copy(others, others, plane_send.at[pair]).wait()
    out_ref[...] = finish(jnp.sum(parts[...], 0))


def run(spec, table, labels, place, mirror, first, twiddle, last):
    vmem = pl.BlockSpec(memory_space=pltpu.VMEM)
    hbm = pl.BlockSpec(memory_space=pl.ANY)
    f32, bf16 = jnp.float32, jnp.bfloat16
    dma = pltpu.SemaphoreType.DMA
    return pl.pallas_call(
        kernel,
        out_shape=pltpu.VMEM((6, 128), f32),
        in_specs=[hbm, hbm] + [vmem] * 6,
        out_specs=vmem,
        scratch_shapes=[
            pltpu.VMEM((6 * MODES, KZ), bf16),
            pltpu.VMEM((4, 512, 2 * HALF), bf16),
            pltpu.VMEM((2, 2, 2 * LANES, 2 * HALF), bf16),
            pltpu.VMEM((ND * ROWS, LANES), f32),
            pltpu.VMEM((2, ND, ROWS, LANES), bf16),
            pltpu.VMEM((2, ND, ROWS, LANES), bf16),
            pltpu.VMEM((ROWS, XW), jnp.int32),
            pltpu.VMEM((512, 8 * LANES), bf16),
            pltpu.VMEM((8 * 256, 2 * LANES), bf16),
            pltpu.VMEM((8 * 256, 2 * LANES), bf16),
            pltpu.VMEM((8, 8 * 256), f32),
            pltpu.VMEM((2, 512, 128), f32),
            pltpu.VMEM((320, XW), bf16),
            pltpu.VMEM((256, XW), bf16),
            pltpu.VMEM((320, XW), bf16),
            pltpu.VMEM((256, XW), bf16),
            pltpu.VMEM((2, 64, 8, 128), f32),
            pltpu.VMEM((64, 8, 128), f32),
            pltpu.VMEM((64, 8, 128), f32),
            pltpu.VMEM((64, 8, 128), f32),
            dma, dma((4,)), dma((2,)), dma((2,)), dma((2,)), dma, dma, dma, dma,
        ],
        compiler_params=pltpu.CompilerParams(
            collective_id=0, has_side_effects=True, vmem_limit_bytes=VMEM_LIMIT
        ),
    )(spec, table, labels, place, mirror, first, twiddle, last)


def finish(centred):
    count, s1, u1, w1, uu, uw, ww = (centred[j] for j in range(7))
    s2 = u1 + 0.5 * s1
    s3 = w1 + 0.5 * s1
    s4 = uu + u1 + 0.25 * s1
    s5 = uw + 0.5 * (u1 + w1) + 0.25 * s1
    s6 = ww + w1 + 0.25 * s1
    weight = jnp.maximum(s1, 1.0)
    centre_x = s2 / weight
    centre_z = s3 / weight
    return jnp.stack(
        [
            s1 / jnp.maximum(count, 1.0),
            centre_x,
            centre_z,
            12.0 * (s4 / weight - centre_x * centre_x),
            12.0 * (s5 / weight - centre_x * centre_z),
            12.0 * (s6 / weight - centre_z * centre_z),
        ],
        0,
    )


def solution(mesh):
    table, mirror = z_tables()
    first, twiddle, last = x_tables()

    def on_device(spectral, labels, block_place):
        spec = spectral.reshape(6 * MODES, KZ)
        out = run(spec, table, labels, block_place.reshape(1, NBLK), mirror, first, twiddle, last)
        return out.reshape(6, 1, 128)

    in_specs = (P(None, None, ("row", "col"), None), P(("row", "col"), None), P())
    return jax.shard_map(on_device, mesh=mesh, in_specs=in_specs, out_specs=P(None, "col", "row"), check_vma=False)
```

```python
import math

import jax
import jax.numpy as jnp
import ml_dtypes
import numpy as np
from jax import lax
from jax.experimental import pallas as pl
from jax.experimental.pallas import tpu as pltpu
from jax.sharding import PartitionSpec as P

KX = 5120
KZ = 7680
NX = 10240
ZW = 2048
XW = 2048
ND = 128
MODES = 40
QK = KZ // 4
HALF = 1024
ROWS = 16
LB = 128
NBLK = 128
LANES = 128
MESH = pl.DeviceIdType.MESH
NT = (((1,), (1,)), ((), ()))
VMEM_LIMIT = 60 * 1024 * 1024


def split(table):
    high = table.astype(ml_dtypes.bfloat16)
    low = (table - high.astype(np.float64)).astype(ml_dtypes.bfloat16)
    return high, low


def z_tables():
    za = np.arange(4)[:, None, None]
    zq = np.arange(4)[None, :, None]
    d = np.arange(ND)[None, None, :]
    z = (16 * d + 4 * zq + za).reshape(4, 512)
    cycle = (np.arange(KZ).astype(np.float32) * np.float32(2.0 * math.pi / KZ)).astype(np.float32)
    phase = (z[:, :, None] * np.arange(HALF)[None, None, :]) % KZ
    kept = np.arange(HALF) <= QK // 2
    cosine = np.where(kept, np.cos(cycle)[phase], 0.0).astype(ml_dtypes.bfloat16)
    sine = np.where(kept, np.sin(cycle)[phase], 0.0).astype(ml_dtypes.bfloat16)
    table = np.concatenate([cosine, sine], 2)
    mirror = np.zeros((2, 256, 128), np.float32)
    lane = np.arange(128)
    mirror[:, 128 - lane, lane] = 1.0
    mirror[1, :, 64] = 0.0
    return table, mirror.astype(ml_dtypes.bfloat16)


def x_tables():
    s = np.arange(ND)
    xa = np.arange(256)
    angle = 2.0 * math.pi * ((xa[:, None] * s[None, :]) % 256) / 256
    real_rows = np.concatenate([np.cos(angle), -np.sin(angle)], 1)
    imag_rows = np.concatenate([np.sin(angle), np.cos(angle)], 1)
    first = np.concatenate(split(np.concatenate([real_rows, imag_rows], 0)), 1)
    m = np.zeros(LANES, np.int64)
    m[: 3 * MODES] = np.arange(3 * MODES) % MODES
    angle = 2.0 * math.pi * (xa[:, None] * m[None, :]) / NX
    twiddle = np.stack([np.cos(angle), np.sin(angle)]).astype(np.float32)
    xb = np.arange(8)
    last = np.zeros((3, 8, 2, LANES))
    for c in range(3):
        angle = 2.0 * math.pi * ((xb[:, None] * np.arange(MODES)[None, :]) % MODES) / MODES
        last[c, :, 0, c * MODES : (c + 1) * MODES] = np.cos(angle)
        last[c, :, 1, c * MODES : (c + 1) * MODES] = -np.sin(angle)
    last = last.reshape(24, 2 * LANES)
    high, low = split(last)
    last = np.concatenate([high, low], 0)
    return first, twiddle, last


def add(p, q):
    return (p[0] + q[0], p[1] + q[1])


def sub(p, q):
    return (p[0] - q[0], p[1] - q[1])


def turn(p):
    return (-p[1], p[0])


def fill(spec, mirror_ref, coef, pair):
    pad = jnp.zeros((LANES - 3 * MODES, 128), jnp.float32)
    for block in range(8):
        turned = []
        for ka in range(4):
            start = ka * QK + (14 - block) * 128
            width = 128 if block == 0 else 256
            matrix = mirror_ref[1 if block == 7 else 0, 0:width, :]
            turned.append(jnp.dot(spec[:, start : start + width], matrix, preferred_element_type=jnp.float32))
        pieces = {}
        for c in range(3):
            near, far = [], []
            for ka in range(4):
                start = ka * QK + block * 128
                x = spec[80 * c : 80 * c + 80, start : start + 128].astype(jnp.float32)
                near.append((x[0:40], x[40:80]))
                far.append((turned[ka][80 * c : 80 * c + 40], turned[ka][80 * c + 40 : 80 * c + 80]))
            sides = []
            for x in (near, far):
                if pair == 0:
                    even, odd = add(x[0], x[2]), add(x[1], x[3])
                else:
                    even, odd = sub(x[0], x[2]), turn(sub(x[1], x[3]))
                sides.append((add(even, odd), sub(even, odd)))
            for zaa in range(2):
                y, r = sides[0][zaa], sides[1][zaa]
                if pair == 1:
                    r = turn(r)
                if zaa == 0:
                    e, o = add(y, r), sub(y, r)
                else:
                    e, o = sub(y, r), add(y, r)
                for name, value in ((0, e[0]), (1, e[1]), (2, -o[1]), (3, o[0])):
                    pieces.setdefault((zaa, name), []).append(value)
        for (zaa, name), values in pieces.items():
            whole = jnp.concatenate(values + [pad], 0)
            rows = slice(name % 2 * LANES, (name % 2 + 1) * LANES)
            cols = slice(name // 2 * HALF + block * 128, name // 2 * HALF + (block + 1) * 128)
            coef[pair, zaa, rows, cols] = whole.astype(jnp.bfloat16)


def plane(tab, coef, wide, msg, pair):
    for zaa in range(2):
        table = tab[pair + 2 * zaa]
        v = lax.dot_general(table, coef[pair, zaa], NT, preferred_element_type=jnp.float32)
        for zq in range(4):
            for part in range(2):
                wide[pl.ds(8 * zaa + 2 * zq + part, ND, stride=ROWS), :] = v[
                    zq * ND : (zq + 1) * ND, part * LANES : (part + 1) * LANES
                ]
    msg[pair] = wide[...].astype(jnp.bfloat16).reshape(ND, ROWS, LANES)


def enstrophy(recv, wide, mats, top, rest, first_ref, tw_ref, last_ref, enst, pair):
    scale = 2.0 / math.sqrt(2.0 * KX * KZ)
    wide[...] = recv[pair].reshape(ND * ROWS, LANES).astype(jnp.float32)
    lane = lax.broadcasted_iota(jnp.int32, (ROWS, LANES), 1)
    factor = jnp.where((lane == 0) | (lane == MODES) | (lane == 2 * MODES), 0.5, 1.0)
    wide[0:ROWS, :] = wide[0:ROWS, :] * factor
    for i in range(8):
        cols = slice(i * LANES, (i + 1) * LANES)
        for part in range(2):
            mat = wide[pl.ds(2 * i + part, ND, stride=ROWS), :].astype(jnp.bfloat16)
            mats[part * ND : (part + 1) * ND, cols] = mat
            mats[(part + 2) * ND : (part + 3) * ND, cols] = mat
    cosine, sine = tw_ref[0], tw_ref[1]
    for two in range(4):
        both = mats[:, two * 256 : (two + 1) * 256]
        y = jnp.dot(first_ref[...], both, preferred_element_type=jnp.float32)
        for half in range(2):
            yr = y[0:256, half * LANES : (half + 1) * LANES]
            yi = y[256:512, half * LANES : (half + 1) * LANES]
            t = jnp.concatenate([yr * cosine - yi * sine, yr * sine + yi * cosine], 1)
            high = t.astype(jnp.bfloat16)
            rows = slice((two * 2 + half) * 256, (two * 2 + half + 1) * 256)
            top[rows, :] = high
            rest[rows, :] = (t - high.astype(jnp.float32)).astype(jnp.bfloat16)
    v = lax.dot_general(last_ref[...], top[...], NT, preferred_element_type=jnp.float32)
    v = v[0:24] + v[24:48]
    v = v + lax.dot_general(last_ref[0:24], rest[...], NT, preferred_element_type=jnp.float32)
    v = v * scale
    enst[...] = v[0:8] * v[0:8] + v[8:16] * v[8:16] + v[16:24] * v[16:24]


def zpoint(pair, i):
    return 4 * (i % 4) + 2 * (i // 4) + pair


def spread(row, count):
    tile = jnp.broadcast_to(row, (16, row.shape[1])).astype(jnp.bfloat16)
    return jnp.concatenate([tile] * (count // 16), 0)


def label_sums(me, targets, enst, acc0, acc1, lhs_a, rhs_a, lhs_b, rhs_b, pair):
    upos = (
        lax.broadcasted_iota(jnp.int32, (8, 256), 0) * 256 + lax.broadcasted_iota(jnp.int32, (8, 256), 1)
    ).astype(jnp.float32) / XW - 0.5
    row64 = lax.broadcasted_iota(jnp.int32, (64, 256), 0).astype(jnp.float32).astype(jnp.bfloat16)
    row256 = lax.broadcasted_iota(jnp.int32, (256, 256), 0).astype(jnp.float32).astype(jnp.bfloat16)
    one = jnp.ones((), jnp.bfloat16)
    zero = jnp.zeros((), jnp.bfloat16)

    def build(i, lhs, rhs):
        z = zpoint(pair, i)
        e = enst[:, pl.ds(pl.multiple_of(i * 256, 256), 256)]
        ehigh = e.astype(jnp.bfloat16).astype(jnp.float32)
        eu = e * upos
        values = [ehigh, e - ehigh, eu, eu * upos]
        for xb in range(8):
            cols = slice(xb * 256, (xb + 1) * 256)
            lab = targets[pl.ds(z, 1), cols]
            hit = spread((lab >> 8).astype(jnp.float32), 64) == row64
            lhs[0:64, cols] = jnp.where(hit, one, zero)
            for j, value in enumerate(values):
                lhs[(j + 1) * 64 : (j + 2) * 64, cols] = jnp.where(hit, spread(value[xb : xb + 1], 64), zero)
            near = spread((lab & 255).astype(jnp.float32), 256) == row256
            rhs[:, cols] = jnp.where(near, one, zero)

    def collect(i, lhs, rhs):
        t = lax.dot_general(lhs[...], rhs[...], NT, preferred_element_type=jnp.float32)
        w = (me * ROWS + zpoint(pair, i)).astype(jnp.float32) / ZW - 0.5
        e_sum = t[64:128] + t[128:192]
        eu_sum = t[192:256]
        terms = [t[0:64], e_sum, eu_sum, e_sum * w, t[256:320], eu_sum * w, e_sum * (w * w)]
        for j, term in enumerate(terms):
            acc0[j * 64 : (j + 1) * 64, :] += term[:, :128]
            acc1[j * 64 : (j + 1) * 64, :] += term[:, 128:]

    buffers = ((lhs_a, rhs_a), (lhs_b, rhs_b))
    build(0, lhs_a, rhs_a)

    def four_rows(n, carry):
        for k in range(4):
            build(4 * n + k + 1 if k < 3 else lax.rem(4 * n + 4, 8), *buffers[(k + 1) % 2])
            collect(4 * n + k, *buffers[k % 2])
        return carry

    lax.fori_loop(0, 2, four_rows, 0)


def kernel(
    spec_hbm, tab_hbm, lab_ref, place_ref, mirror_ref, first_ref, tw_ref, last_ref, out_ref,
    spec, tab, coef, wide, msg, recv, targets, mats, top, rest, enst, acc,
    lhs_a, rhs_a, lhs_b, rhs_b, table, mate, part, parts,
    spec_sem, tab_sem, own_sem, plane_send, plane_recv, pair_send, pair_recv, sum_send, sum_recv,
):
    row = lax.axis_index("row")
    col = lax.axis_index("col")
    me = row * 16 + col
    core = row % 2
    mine = row // 2 * 16 + col
    load = pltpu.make_async_copy(spec_hbm, spec, spec_sem)
    load.start()
    order = (0, 2, 1, 3)
    loads = [pltpu.make_async_copy(tab_hbm.at[za], tab.at[za], tab_sem.at[za]) for za in range(4)]
    barrier = pltpu.get_barrier_semaphore()

    def greet(j, carry):
        d = lax.rem(me + j, ND)
        pl.semaphore_signal(barrier, inc=1, device_id=(d // 16, d % 16), device_id_type=MESH)
        return carry

    lax.fori_loop(1, ND, greet, 0)

    places = jnp.broadcast_to(place_ref[...], (16, LB))
    for i in range(XW // LB):
        cols = slice(i * LB, (i + 1) * LB)
        lab = lab_ref[:, cols]
        targets[:, cols] = jnp.take_along_axis(places, lab >> 7, axis=1) * LB + (lab & 127)
    acc[...] = jnp.zeros_like(acc)

    load.wait()
    for za in order:
        loads[za].start()
    owns = []
    for pair in range(2):
        fill(spec, mirror_ref, coef, pair)
        for zaa in range(2):
            loads[pair + 2 * zaa].wait()
        plane(tab, coef, wide, msg, pair)
        if pair == 0:
            pl.semaphore_wait(barrier, ND - 1)

        def send(j, carry, pair=pair):
            d = lax.rem(me + j, ND)
            pltpu.make_async_remote_copy(
                src_ref=msg.at[pair, d],
                dst_ref=recv.at[pair, me],
                send_sem=plane_send.at[pair],
                recv_sem=plane_recv.at[pair],
                device_id=(d // 16, d % 16),
                device_id_type=MESH,
            ).start()
            return carry

        lax.fori_loop(1, ND, send, 0)
        own = pltpu.make_async_copy(msg.at[pair, me], recv.at[pair, me], own_sem.at[pair])
        own.start()
        owns.append(own)

    for pair in range(2):
        owns[pair].wait()
        others = recv.at[pair, pl.ds(0, ND - 1)]
        pltpu.make_async_copy(others, others, plane_recv.at[pair]).wait()
        enstrophy(recv, wide, mats, top, rest, first_ref, tw_ref, last_ref, enst, pair)
        label_sums(me, targets, enst, acc.at[0], acc.at[1], lhs_a, rhs_a, lhs_b, rhs_b, pair)

    def hand_out(half, there):
        for m in range(16):
            table[half, there * 16 + m] = acc[half, pl.ds(there + 4 * m, 8, stride=64), :]

    theres = [lax.rem(row // 2 + k, 4) for k in (2, 1, 3, 0)]
    swaps = []
    for k, there in enumerate(theres):
        hand_out(1 - core, there)
        blocks = pl.ds(there * 16, 16)
        swap = pltpu.make_async_remote_copy(
            src_ref=table.at[1 - core, blocks],
            dst_ref=mate.at[blocks],
            send_sem=pair_send.at[k],
            recv_sem=pair_recv.at[k],
            device_id=(row + 1 - 2 * core, col),
            device_id_type=MESH,
        )
        swap.start()
        swaps.append(swap)
    for k, there in enumerate(theres):
        hand_out(core, there)
        swaps[k].wait()
        blocks = pl.ds(there * 16, 16)
        part[blocks] = table[core, blocks] + mate[blocks]

        def send_sum(j, carry, there=there):
            c = lax.rem(col + j, 16)
            pltpu.make_async_remote_copy(
                src_ref=part.at[there * 16 + c],
                dst_ref=parts.at[mine],
                send_sem=sum_send,
                recv_sem=sum_recv,
                device_id=(there * 2 + core, c),
                device_id_type=MESH,
            ).start()
            return carry

        lax.fori_loop(1 if k == 3 else 0, 16, send_sum, 0)
    parts[mine] = part[mine]
    every = parts.at[pl.ds(0, 63)]
    pltpu.make_async_copy(every, every, sum_send).wait()
    pltpu.make_async_copy(every, every, sum_recv).wait()
    for pair in range(2):
        others = msg.at[pair, pl.ds(0, ND - 1)]
        pltpu.make_async_copy(others, others, plane_send.at[pair]).wait()
    out_ref[...] = finish(jnp.sum(parts[...], 0))


def run(spec, table, labels, place, mirror, first, twiddle, last):
    vmem = pl.BlockSpec(memory_space=pltpu.VMEM)
    hbm = pl.BlockSpec(memory_space=pl.ANY)
    f32, bf16 = jnp.float32, jnp.bfloat16
    dma = pltpu.SemaphoreType.DMA
    return pl.pallas_call(
        kernel,
        out_shape=pltpu.VMEM((6, 128), f32),
        in_specs=[hbm, hbm] + [vmem] * 6,
        out_specs=vmem,
        scratch_shapes=[
            pltpu.VMEM((6 * MODES, KZ), bf16),
            pltpu.VMEM((4, 512, 2 * HALF), bf16),
            pltpu.VMEM((2, 2, 2 * LANES, 2 * HALF), bf16),
            pltpu.VMEM((ND * ROWS, LANES), f32),
            pltpu.VMEM((2, ND, ROWS, LANES), bf16),
            pltpu.VMEM((2, ND, ROWS, LANES), bf16),
            pltpu.VMEM((ROWS, XW), jnp.int32),
            pltpu.VMEM((512, 8 * LANES), bf16),
            pltpu.VMEM((8 * 256, 2 * LANES), bf16),
            pltpu.VMEM((8 * 256, 2 * LANES), bf16),
            pltpu.VMEM((8, 8 * 256), f32),
            pltpu.VMEM((2, 512, 128), f32),
            pltpu.VMEM((320, XW), bf16),
            pltpu.VMEM((256, XW), bf16),
            pltpu.VMEM((320, XW), bf16),
            pltpu.VMEM((256, XW), bf16),
            pltpu.VMEM((2, 64, 8, 128), f32),
            pltpu.VMEM((64, 8, 128), f32),
            pltpu.VMEM((64, 8, 128), f32),
            pltpu.VMEM((64, 8, 128), f32),
            dma, dma((4,)), dma((2,)), dma((2,)), dma((2,)), dma((4,)), dma((4,)), dma, dma,
        ],
        compiler_params=pltpu.CompilerParams(
            collective_id=0, has_side_effects=True, vmem_limit_bytes=VMEM_LIMIT
        ),
    )(spec, table, labels, place, mirror, first, twiddle, last)


def finish(centred):
    count, s1, u1, w1, uu, uw, ww = (centred[j] for j in range(7))
    s2 = u1 + 0.5 * s1
    s3 = w1 + 0.5 * s1
    s4 = uu + u1 + 0.25 * s1
    s5 = uw + 0.5 * (u1 + w1) + 0.25 * s1
    s6 = ww + w1 + 0.25 * s1
    weight = jnp.maximum(s1, 1.0)
    centre_x = s2 / weight
    centre_z = s3 / weight
    return jnp.stack(
        [
            s1 / jnp.maximum(count, 1.0),
            centre_x,
            centre_z,
            12.0 * (s4 / weight - centre_x * centre_x),
            12.0 * (s5 / weight - centre_x * centre_z),
            12.0 * (s6 / weight - centre_z * centre_z),
        ],
        0,
    )


def solution(mesh):
    table, mirror = z_tables()
    first, twiddle, last = x_tables()

    def on_device(spectral, labels, block_place):
        spec = spectral.reshape(6 * MODES, KZ)
        out = run(spec, table, labels, block_place.reshape(1, NBLK), mirror, first, twiddle, last)
        return out.reshape(6, 1, 128)

    in_specs = (P(None, None, ("row", "col"), None), P(("row", "col"), None), P())
    return jax.shard_map(on_device, mesh=mesh, in_specs=in_specs, out_specs=P(None, "col", "row"), check_vma=False)
```

```python
import math

import jax
import jax.numpy as jnp
import ml_dtypes
import numpy as np
from jax import lax
from jax.experimental import pallas as pl
from jax.experimental.pallas import tpu as pltpu
from jax.sharding import PartitionSpec as P

KX = 5120
KZ = 7680
NX = 10240
ZW = 2048
XW = 2048
ND = 128
MODES = 40
QK = KZ // 4
HALF = 1024
ROWS = 16
LB = 128
NBLK = 128
LANES = 128
MESH = pl.DeviceIdType.MESH
NT = (((1,), (1,)), ((), ()))
VMEM_LIMIT = 60 * 1024 * 1024


def split(table):
    high = table.astype(ml_dtypes.bfloat16)
    low = (table - high.astype(np.float64)).astype(ml_dtypes.bfloat16)
    return high, low


def z_tables():
    za = np.arange(4)[:, None, None]
    zq = np.arange(4)[None, :, None]
    d = np.arange(ND)[None, None, :]
    z = (16 * d + 4 * zq + za).reshape(4, 512)
    cycle = (np.arange(KZ).astype(np.float32) * np.float32(2.0 * math.pi / KZ)).astype(np.float32)
    phase = (z[:, :, None] * np.arange(HALF)[None, None, :]) % KZ
    kept = np.arange(HALF) <= QK // 2
    cosine = np.where(kept, np.cos(cycle)[phase], 0.0).astype(ml_dtypes.bfloat16)
    sine = np.where(kept, np.sin(cycle)[phase], 0.0).astype(ml_dtypes.bfloat16)
    table = np.concatenate([cosine, sine], 2)
    mirror = np.zeros((2, 256, 128), np.float32)
    lane = np.arange(128)
    mirror[:, 128 - lane, lane] = 1.0
    mirror[1, :, 64] = 0.0
    return table, mirror.astype(ml_dtypes.bfloat16)


def x_tables():
    s = np.arange(ND)
    xa = np.arange(256)
    angle = 2.0 * math.pi * ((xa[:, None] * s[None, :]) % 256) / 256
    real_rows = np.concatenate([np.cos(angle), -np.sin(angle)], 1)
    imag_rows = np.concatenate([np.sin(angle), np.cos(angle)], 1)
    first = np.concatenate(split(np.concatenate([real_rows, imag_rows], 0)), 1)
    m = np.zeros(LANES, np.int64)
    m[: 3 * MODES] = np.arange(3 * MODES) % MODES
    angle = 2.0 * math.pi * (xa[:, None] * m[None, :]) / NX
    twiddle = np.stack([np.cos(angle), np.sin(angle)]).astype(np.float32)
    xb = np.arange(8)
    last = np.zeros((3, 8, 2, LANES))
    for c in range(3):
        angle = 2.0 * math.pi * ((xb[:, None] * np.arange(MODES)[None, :]) % MODES) / MODES
        last[c, :, 0, c * MODES : (c + 1) * MODES] = np.cos(angle)
        last[c, :, 1, c * MODES : (c + 1) * MODES] = -np.sin(angle)
    last = last.reshape(24, 2 * LANES)
    high, low = split(last)
    last = np.concatenate([high, low], 0)
    return first, twiddle, last


def add(p, q):
    return (p[0] + q[0], p[1] + q[1])


def sub(p, q):
    return (p[0] - q[0], p[1] - q[1])


def turn(p):
    return (-p[1], p[0])


def fill(spec, mirror_ref, coef, pair):
    pad = jnp.zeros((LANES - 3 * MODES, 128), jnp.float32)
    for block in range(8):
        turned = []
        for ka in range(4):
            start = ka * QK + (14 - block) * 128
            width = 128 if block == 0 else 256
            matrix = mirror_ref[1 if block == 7 else 0, 0:width, :]
            turned.append(jnp.dot(spec[:, start : start + width], matrix, preferred_element_type=jnp.float32))
        pieces = {}
        for c in range(3):
            near, far = [], []
            for ka in range(4):
                start = ka * QK + block * 128
                x = spec[80 * c : 80 * c + 80, start : start + 128].astype(jnp.float32)
                near.append((x[0:40], x[40:80]))
                far.append((turned[ka][80 * c : 80 * c + 40], turned[ka][80 * c + 40 : 80 * c + 80]))
            sides = []
            for x in (near, far):
                if pair == 0:
                    even, odd = add(x[0], x[2]), add(x[1], x[3])
                else:
                    even, odd = sub(x[0], x[2]), turn(sub(x[1], x[3]))
                sides.append((add(even, odd), sub(even, odd)))
            for zaa in range(2):
                y, r = sides[0][zaa], sides[1][zaa]
                if pair == 1:
                    r = turn(r)
                if zaa == 0:
                    e, o = add(y, r), sub(y, r)
                else:
                    e, o = sub(y, r), add(y, r)
                for name, value in ((0, e[0]), (1, e[1]), (2, -o[1]), (3, o[0])):
                    pieces.setdefault((zaa, name), []).append(value)
        for (zaa, name), values in pieces.items():
            whole = jnp.concatenate(values + [pad], 0)
            rows = slice(name % 2 * LANES, (name % 2 + 1) * LANES)
            cols = slice(name // 2 * HALF + block * 128, name // 2 * HALF + (block + 1) * 128)
            coef[pair, zaa, rows, cols] = whole.astype(jnp.bfloat16)


def plane(tab, coef, wide, msg, pair):
    for zaa in range(2):
        table = tab[pair + 2 * zaa]
        v = lax.dot_general(table, coef[pair, zaa], NT, preferred_element_type=jnp.float32)
        for zq in range(4):
            for part in range(2):
                wide[pl.ds(8 * zaa + 2 * zq + part, ND, stride=ROWS), :] = v[
                    zq * ND : (zq + 1) * ND, part * LANES : (part + 1) * LANES
                ]
    msg[pair] = wide[...].astype(jnp.bfloat16).reshape(ND, ROWS, LANES)


def enstrophy(recv, wide, mats, top, rest, first_ref, tw_ref, last_ref, enst, pair):
    scale = 2.0 / math.sqrt(2.0 * KX * KZ)
    wide[...] = recv[pair].reshape(ND * ROWS, LANES).astype(jnp.float32)
    lane = lax.broadcasted_iota(jnp.int32, (ROWS, LANES), 1)
    factor = jnp.where((lane == 0) | (lane == MODES) | (lane == 2 * MODES), 0.5, 1.0)
    wide[0:ROWS, :] = wide[0:ROWS, :] * factor
    for i in range(8):
        cols = slice(i * LANES, (i + 1) * LANES)
        for part in range(2):
            mat = wide[pl.ds(2 * i + part, ND, stride=ROWS), :].astype(jnp.bfloat16)
            mats[part * ND : (part + 1) * ND, cols] = mat
            mats[(part + 2) * ND : (part + 3) * ND, cols] = mat
    cosine, sine = tw_ref[0], tw_ref[1]
    for two in range(4):
        both = mats[:, two * 256 : (two + 1) * 256]
        y = jnp.dot(first_ref[...], both, preferred_element_type=jnp.float32)
        for half in range(2):
            yr = y[0:256, half * LANES : (half + 1) * LANES]
            yi = y[256:512, half * LANES : (half + 1) * LANES]
            t = jnp.concatenate([yr * cosine - yi * sine, yr * sine + yi * cosine], 1)
            high = t.astype(jnp.bfloat16)
            rows = slice((two * 2 + half) * 256, (two * 2 + half + 1) * 256)
            top[rows, :] = high
            rest[rows, :] = (t - high.astype(jnp.float32)).astype(jnp.bfloat16)
    v = lax.dot_general(last_ref[...], top[...], NT, preferred_element_type=jnp.float32)
    v = v[0:24] + v[24:48]
    v = v + lax.dot_general(last_ref[0:24], rest[...], NT, preferred_element_type=jnp.float32)
    v = v * scale
    enst[...] = v[0:8] * v[0:8] + v[8:16] * v[8:16] + v[16:24] * v[16:24]


def zpoint(pair, i):
    return 4 * (i % 4) + 2 * (i // 4) + pair


def spread(row, count):
    tile = jnp.broadcast_to(row, (16, row.shape[1])).astype(jnp.bfloat16)
    return jnp.concatenate([tile] * (count // 16), 0)


def label_sums(me, targets, enst, acc0, acc1, lhs_a, rhs_a, lhs_b, rhs_b, pair):
    upos = (
        lax.broadcasted_iota(jnp.int32, (8, 256), 0) * 256 + lax.broadcasted_iota(jnp.int32, (8, 256), 1)
    ).astype(jnp.float32) / XW - 0.5
    row64 = lax.broadcasted_iota(jnp.int32, (64, 256), 0).astype(jnp.float32).astype(jnp.bfloat16)
    row256 = lax.broadcasted_iota(jnp.int32, (256, 256), 0).astype(jnp.float32).astype(jnp.bfloat16)
    one = jnp.ones((), jnp.bfloat16)
    zero = jnp.zeros((), jnp.bfloat16)

    def build(i, lhs, rhs):
        z = zpoint(pair, i)
        e = enst[:, pl.ds(pl.multiple_of(i * 256, 256), 256)]
        ehigh = e.astype(jnp.bfloat16).astype(jnp.float32)
        eu = e * upos
        values = [ehigh, e - ehigh, eu, eu * upos]
        for xb in range(8):
            cols = slice(xb * 256, (xb + 1) * 256)
            lab = targets[pl.ds(z, 1), cols]
            hit = spread((lab >> 8).astype(jnp.float32), 64) == row64
            lhs[0:64, cols] = jnp.where(hit, one, zero)
            for j, value in enumerate(values):
                lhs[(j + 1) * 64 : (j + 2) * 64, cols] = jnp.where(hit, spread(value[xb : xb + 1], 64), zero)
            near = spread((lab & 255).astype(jnp.float32), 256) == row256
            rhs[:, cols] = jnp.where(near, one, zero)

    def collect(i, lhs, rhs):
        t = lax.dot_general(lhs[...], rhs[...], NT, preferred_element_type=jnp.float32)
        w = (me * ROWS + zpoint(pair, i)).astype(jnp.float32) / ZW - 0.5
        e_sum = t[64:128] + t[128:192]
        eu_sum = t[192:256]
        terms = [t[0:64], e_sum, eu_sum, e_sum * w, t[256:320], eu_sum * w, e_sum * (w * w)]
        for j, term in enumerate(terms):
            acc0[j * 64 : (j + 1) * 64, :] += term[:, :128]
            acc1[j * 64 : (j + 1) * 64, :] += term[:, 128:]

    buffers = ((lhs_a, rhs_a), (lhs_b, rhs_b))
    build(0, lhs_a, rhs_a)

    def four_rows(n, carry):
        for k in range(4):
            build(4 * n + k + 1 if k < 3 else lax.rem(4 * n + 4, 8), *buffers[(k + 1) % 2])
            collect(4 * n + k, *buffers[k % 2])
        return carry

    lax.fori_loop(0, 2, four_rows, 0)


def kernel(
    spec_hbm, tab_hbm, lab_hbm, place_hbm, mirror_hbm, first_hbm, tw_hbm, last_hbm, out_ref,
    lab_ref, place_ref, mirror_ref, first_ref, tw_ref, last_ref, small_sem,
    spec, tab, coef, wide, msg, recv, targets, mats, top, rest, enst, acc,
    lhs_a, rhs_a, lhs_b, rhs_b, table, mate, part, parts,
    spec_sem, tab_sem, own_sem, plane_send, plane_recv, pair_send, pair_recv, sum_send, sum_recv,
):
    row = lax.axis_index("row")
    col = lax.axis_index("col")
    me = row * 16 + col
    core = row % 2
    mine = row // 2 * 16 + col
    load = pltpu.make_async_copy(spec_hbm, spec, spec_sem)
    smalls = [
        pltpu.make_async_copy(source, target, small_sem.at[n])
        for n, (source, target) in enumerate(
            (
                (mirror_hbm, mirror_ref),
                (lab_hbm, lab_ref),
                (place_hbm, place_ref),
                (first_hbm, first_ref),
                (tw_hbm, tw_ref),
                (last_hbm, last_ref),
            )
        )
    ]
    for small in smalls[:3]:
        small.start()
    load.start()
    order = (0, 2, 1, 3)
    loads = [pltpu.make_async_copy(tab_hbm.at[za], tab.at[za], tab_sem.at[za]) for za in range(4)]
    barrier = pltpu.get_barrier_semaphore()

    def greet(j, carry):
        d = lax.rem(me + j, ND)
        pl.semaphore_signal(barrier, inc=1, device_id=(d // 16, d % 16), device_id_type=MESH)
        return carry

    lax.fori_loop(1, ND, greet, 0)

    for small in smalls[:3]:
        small.wait()
    places = jnp.broadcast_to(place_ref[...], (16, LB))
    for i in range(XW // LB):
        cols = slice(i * LB, (i + 1) * LB)
        lab = lab_ref[:, cols]
        targets[:, cols] = jnp.take_along_axis(places, lab >> 7, axis=1) * LB + (lab & 127)
    acc[...] = jnp.zeros_like(acc)

    load.wait()
    for za in order:
        loads[za].start()
    for small in smalls[3:]:
        small.start()
    owns = []
    for pair in range(2):
        fill(spec, mirror_ref, coef, pair)
        for zaa in range(2):
            loads[pair + 2 * zaa].wait()
        plane(tab, coef, wide, msg, pair)
        if pair == 0:
            pl.semaphore_wait(barrier, ND - 1)

        def send(j, carry, pair=pair):
            d = lax.rem(me + j, ND)
            pltpu.make_async_remote_copy(
                src_ref=msg.at[pair, d],
                dst_ref=recv.at[pair, me],
                send_sem=plane_send.at[pair],
                recv_sem=plane_recv.at[pair],
                device_id=(d // 16, d % 16),
                device_id_type=MESH,
            ).start()
            return carry

        lax.fori_loop(1, ND, send, 0)
        own = pltpu.make_async_copy(msg.at[pair, me], recv.at[pair, me], own_sem.at[pair])
        own.start()
        owns.append(own)
    for small in smalls[3:]:
        small.wait()

    for pair in range(2):
        owns[pair].wait()
        others = recv.at[pair, pl.ds(0, ND - 1)]
        pltpu.make_async_copy(others, others, plane_recv.at[pair]).wait()
        enstrophy(recv, wide, mats, top, rest, first_ref, tw_ref, last_ref, enst, pair)
        label_sums(me, targets, enst, acc.at[0], acc.at[1], lhs_a, rhs_a, lhs_b, rhs_b, pair)

    def hand_out(half, there):
        for m in range(16):
            table[half, there * 16 + m] = acc[half, pl.ds(there + 4 * m, 8, stride=64), :]

    theres = [lax.rem(row // 2 + k, 4) for k in (2, 1, 3, 0)]
    swaps = []
    for k, there in enumerate(theres):
        hand_out(1 - core, there)
        blocks = pl.ds(there * 16, 16)
        swap = pltpu.make_async_remote_copy(
            src_ref=table.at[1 - core, blocks],
            dst_ref=mate.at[blocks],
            send_sem=pair_send.at[k],
            recv_sem=pair_recv.at[k],
            device_id=(row + 1 - 2 * core, col),
            device_id_type=MESH,
        )
        swap.start()
        swaps.append(swap)
    for k, there in enumerate(theres):
        hand_out(core, there)
        swaps[k].wait()
        blocks = pl.ds(there * 16, 16)
        part[blocks] = table[core, blocks] + mate[blocks]

        def send_sum(j, carry, there=there):
            c = lax.rem(col + j, 16)
            pltpu.make_async_remote_copy(
                src_ref=part.at[there * 16 + c],
                dst_ref=parts.at[mine],
                send_sem=sum_send,
                recv_sem=sum_recv,
                device_id=(there * 2 + core, c),
                device_id_type=MESH,
            ).start()
            return carry

        lax.fori_loop(1 if k == 3 else 0, 16, send_sum, 0)
    parts[mine] = part[mine]
    every = parts.at[pl.ds(0, 63)]
    pltpu.make_async_copy(every, every, sum_send).wait()
    pltpu.make_async_copy(every, every, sum_recv).wait()
    for pair in range(2):
        others = msg.at[pair, pl.ds(0, ND - 1)]
        pltpu.make_async_copy(others, others, plane_send.at[pair]).wait()
    out_ref[...] = finish(jnp.sum(parts[...], 0))


def run(spec, table, labels, place, mirror, first, twiddle, last):
    vmem = pl.BlockSpec(memory_space=pltpu.VMEM)
    hbm = pl.BlockSpec(memory_space=pl.ANY)
    f32, bf16 = jnp.float32, jnp.bfloat16
    dma = pltpu.SemaphoreType.DMA
    return pl.pallas_call(
        kernel,
        out_shape=pltpu.VMEM((6, 128), f32),
        in_specs=[hbm] * 8,
        out_specs=vmem,
        scratch_shapes=[
            pltpu.VMEM((ROWS, XW), jnp.int32),
            pltpu.VMEM((1, NBLK), jnp.int32),
            pltpu.VMEM(mirror.shape, bf16),
            pltpu.VMEM(first.shape, bf16),
            pltpu.VMEM(twiddle.shape, f32),
            pltpu.VMEM(last.shape, bf16),
            dma((6,)),
            pltpu.VMEM((6 * MODES, KZ), bf16),
            pltpu.VMEM((4, 512, 2 * HALF), bf16),
            pltpu.VMEM((2, 2, 2 * LANES, 2 * HALF), bf16),
            pltpu.VMEM((ND * ROWS, LANES), f32),
            pltpu.VMEM((2, ND, ROWS, LANES), bf16),
            pltpu.VMEM((2, ND, ROWS, LANES), bf16),
            pltpu.VMEM((ROWS, XW), jnp.int32),
            pltpu.VMEM((512, 8 * LANES), bf16),
            pltpu.VMEM((8 * 256, 2 * LANES), bf16),
            pltpu.VMEM((8 * 256, 2 * LANES), bf16),
            pltpu.VMEM((8, 8 * 256), f32),
            pltpu.VMEM((2, 512, 128), f32),
            pltpu.VMEM((320, XW), bf16),
            pltpu.VMEM((256, XW), bf16),
            pltpu.VMEM((320, XW), bf16),
            pltpu.VMEM((256, XW), bf16),
            pltpu.VMEM((2, 64, 8, 128), f32),
            pltpu.VMEM((64, 8, 128), f32),
            pltpu.VMEM((64, 8, 128), f32),
            pltpu.VMEM((64, 8, 128), f32),
            dma, dma((4,)), dma((2,)), dma((2,)), dma((2,)), dma((4,)), dma((4,)), dma, dma,
        ],
        compiler_params=pltpu.CompilerParams(
            collective_id=0, has_side_effects=True, vmem_limit_bytes=VMEM_LIMIT
        ),
    )(spec, table, labels, place, mirror, first, twiddle, last)


def finish(centred):
    count, s1, u1, w1, uu, uw, ww = (centred[j] for j in range(7))
    s2 = u1 + 0.5 * s1
    s3 = w1 + 0.5 * s1
    s4 = uu + u1 + 0.25 * s1
    s5 = uw + 0.5 * (u1 + w1) + 0.25 * s1
    s6 = ww + w1 + 0.25 * s1
    weight = jnp.maximum(s1, 1.0)
    centre_x = s2 / weight
    centre_z = s3 / weight
    return jnp.stack(
        [
            s1 / jnp.maximum(count, 1.0),
            centre_x,
            centre_z,
            12.0 * (s4 / weight - centre_x * centre_x),
            12.0 * (s5 / weight - centre_x * centre_z),
            12.0 * (s6 / weight - centre_z * centre_z),
        ],
        0,
    )


def solution(mesh):
    table, mirror = z_tables()
    first, twiddle, last = x_tables()

    def on_device(spectral, labels, block_place):
        spec = spectral.reshape(6 * MODES, KZ)
        out = run(spec, table, labels, block_place.reshape(1, NBLK), mirror, first, twiddle, last)
        return out.reshape(6, 1, 128)

    in_specs = (P(None, None, ("row", "col"), None), P(("row", "col"), None), P())
    return jax.shard_map(on_device, mesh=mesh, in_specs=in_specs, out_specs=P(None, "col", "row"), check_vma=False)
```

```python
import math

import jax
import jax.numpy as jnp
import ml_dtypes
import numpy as np
from jax import lax
from jax.experimental import pallas as pl
from jax.experimental.pallas import tpu as pltpu
from jax.sharding import PartitionSpec as P

KX = 5120
KZ = 7680
NX = 10240
ZW = 2048
XW = 2048
ND = 128
MODES = 40
QK = KZ // 4
HALF = 1024
ROWS = 16
LB = 128
NBLK = 128
LANES = 128
MESH = pl.DeviceIdType.MESH
NT = (((1,), (1,)), ((), ()))
VMEM_LIMIT = 60 * 1024 * 1024


def split(table):
    high = table.astype(ml_dtypes.bfloat16)
    low = (table - high.astype(np.float64)).astype(ml_dtypes.bfloat16)
    return high, low


def z_tables():
    za = np.arange(4)[:, None, None]
    zq = np.arange(4)[None, :, None]
    d = np.arange(ND)[None, None, :]
    z = (16 * d + 4 * zq + za).reshape(4, 512)
    cycle = (np.arange(KZ).astype(np.float32) * np.float32(2.0 * math.pi / KZ)).astype(np.float32)
    phase = (z[:, :, None] * np.arange(HALF)[None, None, :]) % KZ
    kept = np.arange(HALF) <= QK // 2
    cosine = np.where(kept, np.cos(cycle)[phase], 0.0).astype(ml_dtypes.bfloat16)
    sine = np.where(kept, np.sin(cycle)[phase], 0.0).astype(ml_dtypes.bfloat16)
    table = np.concatenate([cosine, sine], 2)
    mirror = np.zeros((2, 256, 128), np.float32)
    lane = np.arange(128)
    mirror[:, 128 - lane, lane] = 1.0
    mirror[1, :, 64] = 0.0
    return table, mirror.astype(ml_dtypes.bfloat16)


def x_tables():
    s = np.arange(ND)
    xa = np.arange(256)
    angle = 2.0 * math.pi * ((xa[:, None] * s[None, :]) % 256) / 256
    real_rows = np.concatenate([np.cos(angle), -np.sin(angle)], 1)
    imag_rows = np.concatenate([np.sin(angle), np.cos(angle)], 1)
    first = np.concatenate(split(np.concatenate([real_rows, imag_rows], 0)), 1)
    m = np.zeros(LANES, np.int64)
    m[: 3 * MODES] = np.arange(3 * MODES) % MODES
    angle = 2.0 * math.pi * (xa[:, None] * m[None, :]) / NX
    twiddle = np.stack([np.cos(angle), np.sin(angle)]).astype(np.float32)
    xb = np.arange(8)
    last = np.zeros((3, 8, 2, LANES))
    for c in range(3):
        angle = 2.0 * math.pi * ((xb[:, None] * np.arange(MODES)[None, :]) % MODES) / MODES
        last[c, :, 0, c * MODES : (c + 1) * MODES] = np.cos(angle)
        last[c, :, 1, c * MODES : (c + 1) * MODES] = -np.sin(angle)
    last = last.reshape(24, 2 * LANES)
    high, low = split(last)
    last = np.concatenate([high, low], 0)
    return first, twiddle, last


def add(p, q):
    return (p[0] + q[0], p[1] + q[1])


def sub(p, q):
    return (p[0] - q[0], p[1] - q[1])


def turn(p):
    return (-p[1], p[0])


def fill(spec, mirror_ref, coef, pair):
    pad = jnp.zeros((LANES - 3 * MODES, 128), jnp.float32)
    for block in range(8):
        turned = []
        for ka in range(4):
            start = ka * QK + (14 - block) * 128
            width = 128 if block == 0 else 256
            matrix = mirror_ref[1 if block == 7 else 0, 0:width, :]
            turned.append(jnp.dot(spec[:, start : start + width], matrix, preferred_element_type=jnp.float32))
        pieces = {}
        for c in range(3):
            near, far = [], []
            for ka in range(4):
                start = ka * QK + block * 128
                x = spec[80 * c : 80 * c + 80, start : start + 128].astype(jnp.float32)
                near.append((x[0:40], x[40:80]))
                far.append((turned[ka][80 * c : 80 * c + 40], turned[ka][80 * c + 40 : 80 * c + 80]))
            sides = []
            for x in (near, far):
                if pair == 0:
                    even, odd = add(x[0], x[2]), add(x[1], x[3])
                else:
                    even, odd = sub(x[0], x[2]), turn(sub(x[1], x[3]))
                sides.append((add(even, odd), sub(even, odd)))
            for zaa in range(2):
                y, r = sides[0][zaa], sides[1][zaa]
                if pair == 1:
                    r = turn(r)
                if zaa == 0:
                    e, o = add(y, r), sub(y, r)
                else:
                    e, o = sub(y, r), add(y, r)
                for name, value in ((0, e[0]), (1, e[1]), (2, -o[1]), (3, o[0])):
                    pieces.setdefault((zaa, name), []).append(value)
        for (zaa, name), values in pieces.items():
            whole = jnp.concatenate(values + [pad], 0)
            rows = slice(name % 2 * LANES, (name % 2 + 1) * LANES)
            cols = slice(name // 2 * HALF + block * 128, name // 2 * HALF + (block + 1) * 128)
            coef[pair, zaa, rows, cols] = whole.astype(jnp.bfloat16)


def plane(tab, coef, wide, msg, pair):
    for zaa in range(2):
        table = tab[pair + 2 * zaa]
        v = lax.dot_general(table, coef[pair, zaa], NT, preferred_element_type=jnp.float32)
        for zq in range(4):
            for part in range(2):
                wide[pl.ds(8 * zaa + 2 * zq + part, ND, stride=ROWS), :] = v[
                    zq * ND : (zq + 1) * ND, part * LANES : (part + 1) * LANES
                ]
    msg[pair] = wide[...].astype(jnp.bfloat16).reshape(ND, ROWS, LANES)


def enstrophy(recv, wide, mats, top, rest, first_ref, tw_ref, last_ref, enst, pair):
    scale = 2.0 / math.sqrt(2.0 * KX * KZ)
    wide[...] = recv[pair].reshape(ND * ROWS, LANES).astype(jnp.float32)
    lane = lax.broadcasted_iota(jnp.int32, (ROWS, LANES), 1)
    factor = jnp.where((lane == 0) | (lane == MODES) | (lane == 2 * MODES), 0.5, 1.0)
    wide[0:ROWS, :] = wide[0:ROWS, :] * factor
    for i in range(8):
        cols = slice(i * LANES, (i + 1) * LANES)
        for part in range(2):
            mat = wide[pl.ds(2 * i + part, ND, stride=ROWS), :].astype(jnp.bfloat16)
            mats[part * ND : (part + 1) * ND, cols] = mat
            mats[(part + 2) * ND : (part + 3) * ND, cols] = mat
    cosine, sine = tw_ref[0], tw_ref[1]
    for two in range(4):
        both = mats[:, two * 256 : (two + 1) * 256]
        y = jnp.dot(first_ref[...], both, preferred_element_type=jnp.float32)
        for half in range(2):
            yr = y[0:256, half * LANES : (half + 1) * LANES]
            yi = y[256:512, half * LANES : (half + 1) * LANES]
            t = jnp.concatenate([yr * cosine - yi * sine, yr * sine + yi * cosine], 1)
            high = t.astype(jnp.bfloat16)
            rows = slice((two * 2 + half) * 256, (two * 2 + half + 1) * 256)
            top[rows, :] = high
            rest[rows, :] = (t - high.astype(jnp.float32)).astype(jnp.bfloat16)
    v = lax.dot_general(last_ref[...], top[...], NT, preferred_element_type=jnp.float32)
    v = v[0:24] + v[24:48]
    v = v + lax.dot_general(last_ref[0:24], rest[...], NT, preferred_element_type=jnp.float32)
    v = v * scale
    enst[...] = v[0:8] * v[0:8] + v[8:16] * v[8:16] + v[16:24] * v[16:24]


def zpoint(pair, i):
    return 4 * (i % 4) + 2 * (i // 4) + pair


def spread(row, count):
    tile = jnp.broadcast_to(row, (16, row.shape[1])).astype(jnp.bfloat16)
    return jnp.concatenate([tile] * (count // 16), 0)


def label_sums(me, targets, enst, acc0, acc1, lhs_a, rhs_a, lhs_b, rhs_b, pair):
    upos = (
        lax.broadcasted_iota(jnp.int32, (8, 256), 0) * 256 + lax.broadcasted_iota(jnp.int32, (8, 256), 1)
    ).astype(jnp.float32) / XW - 0.5
    row64 = lax.broadcasted_iota(jnp.int32, (64, 256), 0).astype(jnp.float32).astype(jnp.bfloat16)
    row256 = lax.broadcasted_iota(jnp.int32, (256, 256), 0).astype(jnp.float32).astype(jnp.bfloat16)
    one = jnp.ones((), jnp.bfloat16)
    zero = jnp.zeros((), jnp.bfloat16)

    def build(i, lhs, rhs):
        z = zpoint(pair, i)
        e = enst[:, pl.ds(pl.multiple_of(i * 256, 256), 256)]
        ehigh = e.astype(jnp.bfloat16).astype(jnp.float32)
        eu = e * upos
        values = [ehigh, e - ehigh, eu, eu * upos]
        for xb in range(8):
            cols = slice(xb * 256, (xb + 1) * 256)
            lab = targets[pl.ds(z, 1), cols]
            hit = spread((lab >> 8).astype(jnp.float32), 64) == row64
            lhs[0:64, cols] = jnp.where(hit, one, zero)
            for j, value in enumerate(values):
                lhs[(j + 1) * 64 : (j + 2) * 64, cols] = jnp.where(hit, spread(value[xb : xb + 1], 64), zero)
            near = spread((lab & 255).astype(jnp.float32), 256) == row256
            rhs[:, cols] = jnp.where(near, one, zero)

    def collect(i, lhs, rhs):
        t = lax.dot_general(lhs[...], rhs[...], NT, preferred_element_type=jnp.float32)
        w = (me * ROWS + zpoint(pair, i)).astype(jnp.float32) / ZW - 0.5
        e_sum = t[64:128] + t[128:192]
        eu_sum = t[192:256]
        terms = [t[0:64], e_sum, eu_sum, e_sum * w, t[256:320], eu_sum * w, e_sum * (w * w)]
        for j, term in enumerate(terms):
            acc0[j * 64 : (j + 1) * 64, :] += term[:, :128]
            acc1[j * 64 : (j + 1) * 64, :] += term[:, 128:]

    buffers = ((lhs_a, rhs_a), (lhs_b, rhs_b))
    build(0, lhs_a, rhs_a)

    def four_rows(n, carry):
        for k in range(4):
            build(4 * n + k + 1 if k < 3 else lax.rem(4 * n + 4, 8), *buffers[(k + 1) % 2])
            collect(4 * n + k, *buffers[k % 2])
        return carry

    lax.fori_loop(0, 2, four_rows, 0)


def kernel(
    spec_hbm, tab_hbm, lab_hbm, place_hbm, mirror_hbm, first_hbm, tw_hbm, last_hbm, out_ref,
    lab_ref, place_ref, mirror_ref, first_ref, tw_ref, last_ref, small_sem,
    spec, tab, coef, wide, msg, recv, targets, mats, top, rest, enst, acc,
    lhs_a, rhs_a, lhs_b, rhs_b, table, mate, part, parts,
    spec_sem, tab_sem, own_sem, plane_send, plane_recv, pair_send, pair_recv, sum_send, sum_recv,
):
    row = lax.axis_index("row")
    col = lax.axis_index("col")
    me = row * 16 + col
    core = row % 2
    mine = row // 2 * 16 + col
    load = pltpu.make_async_copy(spec_hbm, spec, spec_sem)
    smalls = [
        pltpu.make_async_copy(source, target, small_sem.at[n])
        for n, (source, target) in enumerate(
            (
                (mirror_hbm, mirror_ref),
                (lab_hbm, lab_ref),
                (place_hbm, place_ref),
                (first_hbm, first_ref),
                (tw_hbm, tw_ref),
                (last_hbm, last_ref),
            )
        )
    ]
    for small in smalls[:3]:
        small.start()
    load.start()
    order = (0, 2, 1, 3)
    loads = [pltpu.make_async_copy(tab_hbm.at[za], tab.at[za], tab_sem.at[za]) for za in range(4)]
    barrier = pltpu.get_barrier_semaphore()

    def greet(j, carry):
        d = lax.rem(me + j, ND)
        pl.semaphore_signal(barrier, inc=1, device_id=(d // 16, d % 16), device_id_type=MESH)
        return carry

    lax.fori_loop(1, ND, greet, 0)

    smalls[0].wait()
    load.wait()
    for za in order:
        loads[za].start()
    for small in smalls[3:]:
        small.start()
    owns = []
    for pair in range(2):
        fill(spec, mirror_ref, coef, pair)
        for zaa in range(2):
            loads[pair + 2 * zaa].wait()
        plane(tab, coef, wide, msg, pair)
        if pair == 0:
            pl.semaphore_wait(barrier, ND - 1)

        def send(j, carry, pair=pair):
            d = lax.rem(me + j, ND)
            pltpu.make_async_remote_copy(
                src_ref=msg.at[pair, d],
                dst_ref=recv.at[pair, me],
                send_sem=plane_send.at[pair],
                recv_sem=plane_recv.at[pair],
                device_id=(d // 16, d % 16),
                device_id_type=MESH,
            ).start()
            return carry

        lax.fori_loop(1, ND, send, 0)
        own = pltpu.make_async_copy(msg.at[pair, me], recv.at[pair, me], own_sem.at[pair])
        own.start()
        owns.append(own)
    for small in smalls[1:]:
        small.wait()
    places = jnp.broadcast_to(place_ref[...], (16, LB))
    for i in range(XW // LB):
        cols = slice(i * LB, (i + 1) * LB)
        lab = lab_ref[:, cols]
        targets[:, cols] = jnp.take_along_axis(places, lab >> 7, axis=1) * LB + (lab & 127)
    acc[...] = jnp.zeros_like(acc)

    for pair in range(2):
        owns[pair].wait()
        others = recv.at[pair, pl.ds(0, ND - 1)]
        pltpu.make_async_copy(others, others, plane_recv.at[pair]).wait()
        enstrophy(recv, wide, mats, top, rest, first_ref, tw_ref, last_ref, enst, pair)
        label_sums(me, targets, enst, acc.at[0], acc.at[1], lhs_a, rhs_a, lhs_b, rhs_b, pair)

    def hand_out(half, there):
        for m in range(16):
            table[half, there * 16 + m] = acc[half, pl.ds(there + 4 * m, 8, stride=64), :]

    theres = [lax.rem(row // 2 + k, 4) for k in (2, 1, 3, 0)]
    swaps = []
    for k, there in enumerate(theres):
        hand_out(1 - core, there)
        blocks = pl.ds(there * 16, 16)
        swap = pltpu.make_async_remote_copy(
            src_ref=table.at[1 - core, blocks],
            dst_ref=mate.at[blocks],
            send_sem=pair_send.at[k],
            recv_sem=pair_recv.at[k],
            device_id=(row + 1 - 2 * core, col),
            device_id_type=MESH,
        )
        swap.start()
        swaps.append(swap)
    for k, there in enumerate(theres):
        hand_out(core, there)
        swaps[k].wait()
        blocks = pl.ds(there * 16, 16)
        part[blocks] = table[core, blocks] + mate[blocks]

        def send_sum(j, carry, there=there):
            c = lax.rem(col + j, 16)
            pltpu.make_async_remote_copy(
                src_ref=part.at[there * 16 + c],
                dst_ref=parts.at[mine],
                send_sem=sum_send,
                recv_sem=sum_recv,
                device_id=(there * 2 + core, c),
                device_id_type=MESH,
            ).start()
            return carry

        lax.fori_loop(1 if k == 3 else 0, 16, send_sum, 0)
    parts[mine] = part[mine]
    every = parts.at[pl.ds(0, 63)]
    pltpu.make_async_copy(every, every, sum_send).wait()
    pltpu.make_async_copy(every, every, sum_recv).wait()
    for pair in range(2):
        others = msg.at[pair, pl.ds(0, ND - 1)]
        pltpu.make_async_copy(others, others, plane_send.at[pair]).wait()
    out_ref[...] = finish(jnp.sum(parts[...], 0))


def run(spec, table, labels, place, mirror, first, twiddle, last):
    vmem = pl.BlockSpec(memory_space=pltpu.VMEM)
    hbm = pl.BlockSpec(memory_space=pl.ANY)
    f32, bf16 = jnp.float32, jnp.bfloat16
    dma = pltpu.SemaphoreType.DMA
    return pl.pallas_call(
        kernel,
        out_shape=pltpu.VMEM((6, 128), f32),
        in_specs=[hbm] * 8,
        out_specs=vmem,
        scratch_shapes=[
            pltpu.VMEM((ROWS, XW), jnp.int32),
            pltpu.VMEM((1, NBLK), jnp.int32),
            pltpu.VMEM(mirror.shape, bf16),
            pltpu.VMEM(first.shape, bf16),
            pltpu.VMEM(twiddle.shape, f32),
            pltpu.VMEM(last.shape, bf16),
            dma((6,)),
            pltpu.VMEM((6 * MODES, KZ), bf16),
            pltpu.VMEM((4, 512, 2 * HALF), bf16),
            pltpu.VMEM((2, 2, 2 * LANES, 2 * HALF), bf16),
            pltpu.VMEM((ND * ROWS, LANES), f32),
            pltpu.VMEM((2, ND, ROWS, LANES), bf16),
            pltpu.VMEM((2, ND, ROWS, LANES), bf16),
            pltpu.VMEM((ROWS, XW), jnp.int32),
            pltpu.VMEM((512, 8 * LANES), bf16),
            pltpu.VMEM((8 * 256, 2 * LANES), bf16),
            pltpu.VMEM((8 * 256, 2 * LANES), bf16),
            pltpu.VMEM((8, 8 * 256), f32),
            pltpu.VMEM((2, 512, 128), f32),
            pltpu.VMEM((320, XW), bf16),
            pltpu.VMEM((256, XW), bf16),
            pltpu.VMEM((320, XW), bf16),
            pltpu.VMEM((256, XW), bf16),
            pltpu.VMEM((2, 64, 8, 128), f32),
            pltpu.VMEM((64, 8, 128), f32),
            pltpu.VMEM((64, 8, 128), f32),
            pltpu.VMEM((64, 8, 128), f32),
            dma, dma((4,)), dma((2,)), dma((2,)), dma((2,)), dma((4,)), dma((4,)), dma, dma,
        ],
        compiler_params=pltpu.CompilerParams(
            collective_id=0, has_side_effects=True, vmem_limit_bytes=VMEM_LIMIT
        ),
    )(spec, table, labels, place, mirror, first, twiddle, last)


def finish(centred):
    count, s1, u1, w1, uu, uw, ww = (centred[j] for j in range(7))
    s2 = u1 + 0.5 * s1
    s3 = w1 + 0.5 * s1
    s4 = uu + u1 + 0.25 * s1
    s5 = uw + 0.5 * (u1 + w1) + 0.25 * s1
    s6 = ww + w1 + 0.25 * s1
    weight = jnp.maximum(s1, 1.0)
    centre_x = s2 / weight
    centre_z = s3 / weight
    return jnp.stack(
        [
            s1 / jnp.maximum(count, 1.0),
            centre_x,
            centre_z,
            12.0 * (s4 / weight - centre_x * centre_x),
            12.0 * (s5 / weight - centre_x * centre_z),
            12.0 * (s6 / weight - centre_z * centre_z),
        ],
        0,
    )


def solution(mesh):
    table, mirror = z_tables()
    first, twiddle, last = x_tables()

    def on_device(spectral, labels, block_place):
        spec = spectral.reshape(6 * MODES, KZ)
        out = run(spec, table, labels, block_place.reshape(1, NBLK), mirror, first, twiddle, last)
        return out.reshape(6, 1, 128)

    in_specs = (P(None, None, ("row", "col"), None), P(("row", "col"), None), P())
    return jax.shard_map(on_device, mesh=mesh, in_specs=in_specs, out_specs=P(None, "col", "row"), check_vma=False)
```
